32 devices in a mesh: dp: 4 (over z), fsdp: 8 (over y, x, core).
Axes of the slice: x: 2, y: 2, z: 4, core: 2. Of those that a mesh axis runs over, the one named last changes fastest.
Arguments:
- gate_act: bfloat16 [2048, 14848], P('fsdp', 'dp'), may hold values from -6 to 6
- up_act: bfloat16 [2048, 14848], P('fsdp', 'dp'), may hold values from -6 to 6
- out_grad: bfloat16 [2048, 4096], P('fsdp'), may hold values from -6 to 6
- master_old: float32 [4, 4992, 4096], P('dp', 'fsdp'), may hold values from -0.046875 to 0.046875
- moment1_old: float32 [4, 4992, 4096], P('dp', 'fsdp'), may hold values from -4 to 4
- moment2_old: float32 [4, 4992, 4096], P('dp', 'fsdp'), may hold values from 0.02 to 4
- old_bounds: int32 [4, 9], P('dp'), may hold values from 0 to 3712, as said below
- new_bounds: int32 [4, 8], P('dp'), may hold values from 0 to 3712, as said below
- rank_map: int32 [4, 8], P('dp'), may hold values from 0 to 7, as said below
Outputs:
- mlp_out: float32 [2048, 4096], P('fsdp', 'dp')
- master_new: float32 [4, 4992, 4096], P('dp', 'fsdp')
- moment1_new: float32 [4, 4992, 4096], P('dp', 'fsdp')
- moment2_new: float32 [4, 4992, 4096], P('dp', 'fsdp')
The draws below stay inside these ranges and needn't reach their ends.
Inputs may be any that keep to these rules, and one draw needn't show every extreme that they name: Each row of old_bounds starts at 0, ends at 3712 and never falls; each position's rows fit its 624 slots. Each row of new_bounds starts at 0, ends at 3712 and never falls; each rank's rows fit 624 slots. In every block a position's new rows lie within its old rows and at most 232 rows of each of its two neighbours. `rank_map`: in each block's row exactly one position, one of the two middle ones, has rank 8 - 1 and owns nothing; the others hold the ranks 0 to 6 in position order.
All inputs are finite; a program needn't handle non-finite values.
Results may differ from the reference program's by a relative error of at most 0.012.
Values may be sent and summed in bfloat16 or wider, within the bound.
No kernel may reach another device: no remote copies, remote signals or barrier semaphores. Data moves between devices by JAX's collectives and lax.ppermute only.
A program may use at most 384 MiB of HBM per device.

```python
import math
import jax
import jax.numpy as jnp
from jax import lax

D = 4096
FF = 14848
TOK_DEV = 256
TOKENS = 2048
HID = 3712
CAP = 624
N_DP = 4
N_FSDP = 8


def block_layout(key, block):
    ranks_total = N_FSDP
    block_rows = FF // N_DP
    base_rows = block_rows // ranks_total
    key_bump, key_lost, key_edge = jax.random.split(jax.random.fold_in(key, 100 + block), 3)
    lost_slot = ranks_total // 2 - 1 + jax.random.randint(key_lost, (), 0, 2)
    rank_index = jnp.arange(ranks_total)
    bump_values = jax.random.randint(key_bump, (ranks_total,), 0, 2)
    bump_values = jnp.where(rank_index == lost_slot, jnp.roll(bump_values, 1), bump_values)
    row_counts = base_rows + bump_values - jnp.roll(bump_values, 1)
    old_bounds = jnp.concatenate([jnp.zeros((1,), jnp.int32), jnp.cumsum(row_counts).astype(jnp.int32)])
    left_share = base_rows // 2
    right_share = base_rows - left_share
    position = jnp.arange(ranks_total + 1)
    left_shift = left_share * position // lost_slot
    right_shift = -(right_share * (ranks_total - position) // (ranks_total - 1 - lost_slot))
    shift = jnp.where(position <= lost_slot, left_shift, right_shift)
    edge = jax.random.randint(key_edge, (2,), 1, 3)
    sign = 1 if block % 2 == 0 else -1
    shift = jnp.where(position == 1, sign * edge[0], shift)
    shift = jnp.where(position == ranks_total - 1, sign * edge[1], shift)
    boundary = old_bounds + shift
    new_bounds = jnp.where(rank_index < lost_slot, boundary[:ranks_total], boundary[1:])
    rank_map = jnp.where(rank_index < lost_slot, rank_index, jnp.where(rank_index == lost_slot, ranks_total - 1, rank_index - 1))
    return (old_bounds.astype(jnp.int32), new_bounds.astype(jnp.int32), rank_map.astype(jnp.int32))


def layout_ints(key):
    pieces = [block_layout(key, block) for block in range(N_DP)]
    return tuple((jnp.stack([piece[index] for piece in pieces]) for index in range(3)))


def draw_old_bounds(key, part):
    return layout_ints(key)[0]


def draw_new_bounds(key, part):
    return layout_ints(key)[1]


def draw_rank_map(key, part):
    return layout_ints(key)[2]


def block_levels(key, dims, cuts, least, high):
    factor_of = 1.0
    for dim, parts in cuts:
        steps = jax.random.uniform(jax.random.fold_in(jax.random.fold_in(key, 6), dim), (parts,), jnp.float32, least / len(cuts), high / len(cuts))
        factor_of = factor_of * jnp.repeat(jnp.exp(steps), dims[dim] // parts).reshape((-1,) + (1,) * (len(dims) - 1 - dim))
    return factor_of


def centred(own_key, extent, deviation, limit, cuts=(), kind=jnp.bfloat16):
    array = jax.random.normal(own_key, extent, jnp.float32) * deviation
    if len(cuts) > 0:
        array = block_levels(own_key, extent, cuts, -0.22, 0.18) * array
    return jnp.clip(array, min=-limit, max=limit).astype(kind)


def setup_inputs(seed: int = 0) -> dict:
    key_of = jax.random.split(jax.random.key(seed), 10)
    gate_act = centred(key_of[0], (TOKENS, FF), 1.0, 6.0, ((0, 8), (1, 4)))
    up_act = centred(key_of[1], (TOKENS, FF), 1.0, 6.0, ((0, 8), (1, 4)))
    out_grad = centred(key_of[2], (TOKENS, D), 1.0, 6.0, ((0, 8),))
    master_old = centred(key_of[3], (N_DP, N_FSDP * CAP, D), FF ** -0.5, 0.046875, ((0, 4), (1, 8)), jnp.float32)
    moment1_old = centred(key_of[4], (N_DP, N_FSDP * CAP, D), 0.6, 4.0, ((0, 4), (1, 8)), jnp.float32)
    moment2_old = jnp.clip(jnp.exp(math.log(4.0) - 5.2983174 * jax.random.uniform(key_of[5], (N_DP, N_FSDP * CAP, D), jnp.float32) ** block_levels(key_of[5], (N_DP, N_FSDP * CAP, D), ((0, 4), (1, 8)), -0.2, 0.2)), 0.02, 4.0)
    old_bounds = draw_old_bounds(jax.random.fold_in(key_of[9], 71), 0)
    new_bounds = draw_new_bounds(jax.random.fold_in(key_of[9], 71), 0)
    rank_map = draw_rank_map(jax.random.fold_in(key_of[9], 71), 0)
    return dict(gate_act=gate_act, up_act=up_act, out_grad=out_grad, master_old=master_old, moment1_old=moment1_old, moment2_old=moment2_old, old_bounds=old_bounds, new_bounds=new_bounds, rank_map=rank_map)


def reference(gate_act, up_act, out_grad, master_old, moment1_old, moment2_old, old_bounds, new_bounds, rank_map):
    rows = jnp.arange(HID, dtype=jnp.int32)
    masters = []
    firsts = []
    seconds = []
    for block in range(N_DP):
        bounds = old_bounds[block]
        owner = lax.optimization_barrier(jnp.sum((bounds[1:][None, :] <= rows[:, None]).astype(jnp.int32), axis=1)).astype(jnp.int32)
        slot = (owner * CAP + rows - bounds[owner]).astype(jnp.int32)
        masters.append(jnp.take(master_old[block], slot, axis=0))
        firsts.append(jnp.take(moment1_old[block], slot, axis=0))
        seconds.append(jnp.take(moment2_old[block], slot, axis=0))
    weight_master = jnp.stack(masters)
    moment_first = jnp.stack(firsts)
    moment_second = jnp.stack(seconds)
    weight_low = weight_master.astype(jnp.bfloat16)
    hidden = (jax.nn.silu(gate_act.astype(jnp.float32)) * up_act.astype(jnp.float32)).astype(jnp.bfloat16)
    total = jnp.zeros((TOKENS, D), jnp.float32)
    for block in range(N_DP):
        part = jnp.dot(hidden[:, block * HID:(block + 1) * HID], weight_low[block], preferred_element_type=jnp.float32)
        rounded = lax.optimization_barrier(part.astype(jnp.bfloat16))
        total = total + rounded.astype(jnp.float32)
    mlp_out = total
    grouped_hidden = hidden.reshape(N_FSDP, TOK_DEV, FF)
    grouped_grad = out_grad.reshape(N_FSDP, TOK_DEV, D)

    def accumulate(carry, pair):
        hidden_part, grad_part = pair
        term = jnp.dot(hidden_part.T, grad_part, preferred_element_type=jnp.float32).astype(jnp.bfloat16)
        return (carry + term.astype(jnp.float32), None)
    summed, _ = lax.scan(accumulate, jnp.zeros((FF, D), jnp.float32), (grouped_hidden, grouped_grad))
    grad = (summed * (1.0 / math.sqrt(TOKENS))).reshape(N_DP, HID, D)
    first_next = 0.9 * moment_first + 0.1 * grad
    second_next = 0.95 * moment_second + 0.05 * grad * grad
    master_next = weight_master - 0.001 * (first_next / (jnp.sqrt(second_next) + 1e-08) + 0.1 * weight_master)
    slots = jnp.arange(N_FSDP * CAP, dtype=jnp.int32)
    position = slots // CAP
    within = slots % CAP
    out_master = []
    out_first = []
    out_second = []
    for block in range(N_DP):
        new_rank = rank_map[block][position]
        extended = jnp.concatenate([new_bounds[block], new_bounds[block][-1:]])
        start_row = extended[new_rank]
        live_rows = extended[new_rank + 1] - start_row
        valid = within < live_rows
        source = jnp.clip(start_row + within, 0, HID - 1).astype(jnp.int32)

        def placed(values):
            chosen = jnp.take(values, source, axis=0)
            return jnp.where(valid[:, None], chosen, jnp.zeros_like(chosen))
        out_master.append(placed(master_next[block]))
        out_first.append(placed(first_next[block]))
        out_second.append(placed(second_next[block]))
    return (mlp_out, jnp.stack(out_master), jnp.stack(out_first), jnp.stack(out_second))
```

```python
import functools
import math

import jax
import jax.numpy as jnp
from jax import lax
from jax.experimental import pallas as pl
from jax.experimental.pallas import tpu as pltpu
from jax.sharding import PartitionSpec as P

BF16 = jnp.bfloat16
F32 = jnp.float32
VMEM_BYTES = 58 * 1024 * 1024
SMEM = pl.BlockSpec(memory_space=pltpu.SMEM)


def round_up(value, step):
    return -(-value // step) * step


def params():
    return pltpu.CompilerParams(vmem_limit_bytes=VMEM_BYTES)


def cost(flops, moved):
    return pl.CostEstimate(flops=int(flops), bytes_accessed=int(moved), transcendentals=0)


def old_range(tab, n, q):
    return tab[q], tab[q + 1]


def new_range(tab, n, q):
    k = tab[2 * n + 1 + q]
    return tab[n + 1 + jnp.minimum(k, n - 1)], tab[n + 1 + jnp.minimum(k + 1, n - 1)]


def shifted_rows(ref, start, rows):
    base = pl.multiple_of((start // 8) * 8, 8)
    rem = start - base
    x = ref[pl.ds(base, rows + 8), :]
    lanes = x.shape[1]
    y = pltpu.roll(x.reshape(rows // 8 + 1, 8, lanes), (8 - rem) % 8, 1)
    sublane = lax.broadcasted_iota(jnp.int32, (rows // 8, 8, lanes), 1)
    return jnp.where(sublane < 8 - rem, y[:-1], y[1:]).reshape(rows, lanes)


def place_rows(ref, x, start):
    rows, lanes = x.shape
    base = pl.multiple_of((start // 8) * 8, 8)
    rem = start - base
    y = pltpu.roll(x.reshape(rows // 8, 8, lanes), rem, 1)
    before = jnp.concatenate([y[:1], y])
    after = jnp.concatenate([y, y[-1:]])
    sublane = lax.broadcasted_iota(jnp.int32, (rows // 8 + 1, 8, lanes), 1)
    merged = jnp.where(sublane < rem, before, after).reshape(rows + 8, lanes)
    row = lax.broadcasted_iota(jnp.int32, (rows + 8, lanes), 0)
    ref[pl.ds(base, rows + 8), :] = jnp.where(row >= rem, merged, ref[pl.ds(base, rows + 8), :])


def relayout(tab, n, own, left, right, src, dst):
    slot, mv = own.shape[0], left.shape[0]
    q = tab[3 * n + 1]
    old_start, old_end = old_range(tab, n, q)
    new_start, _ = new_range(tab, n, q)
    src[0:mv, :] = left.astype(F32)
    src[mv : mv + slot, :] = own
    start = mv + jnp.clip(new_start - old_start, -mv, slot)
    dst[mv : mv + slot, :] = shifted_rows(src, start, slot)
    place_rows(dst, right.astype(F32), mv + jnp.clip(old_end - new_start, -mv, slot))


def hidden_kernel(n, rows, tab, gate, up, *refs):
    outs, scratch = refs[:-1], refs[-1]
    tokens, width = gate.shape
    for first in range(0, width, 128):
        last = min(first + 128, width)
        g = gate[:, first:last].astype(F32)
        h = g / (1.0 + jnp.exp(-g)) * up[:, first:last].astype(F32)
        scratch[first:last, :] = h.T
    scratch[width:, :] = jnp.zeros((scratch.shape[0] - width, tokens), F32)
    q = tab[3 * n + 1]
    for rel, out in enumerate(outs):
        for other in range(2):
            start, _ = new_range(tab, n, q ^ (2 * rel + other))
            out[other] = shifted_rows(scratch, start, rows).astype(BF16)


def hidden_windows(tab, gate, up, n, rows):
    tokens, width = gate.shape
    shape = jax.ShapeDtypeStruct((2, rows, tokens), BF16)
    return pl.pallas_call(
        functools.partial(hidden_kernel, n, rows),
        out_shape=[shape] * (n // 2),
        in_specs=[SMEM, pl.BlockSpec(memory_space=pltpu.VMEM), pl.BlockSpec(memory_space=pltpu.VMEM)],
        out_specs=[pl.BlockSpec(memory_space=pltpu.VMEM)] * (n // 2),
        scratch_shapes=[pltpu.VMEM((round_up(width, 8) + rows + 8, tokens), F32)],
        compiler_params=params(),
        cost_estimate=cost(0, 25e6),
    )(tab, gate, up)


def edges_kernel(n, mv, count, tab, *refs):
    ins, outs, scratch = refs[:count], refs[count : 3 * count], refs[-1]
    q = tab[3 * n + 1]
    old_start, old_end = old_range(tab, n, q)
    live = old_end - old_start
    slot = ins[0].shape[0]
    base = pl.multiple_of((jnp.clip(live - mv, 0, slot - mv - 8) // 8) * 8, 8)
    for i in range(count):
        outs[2 * i][...] = ins[i][0:mv, :].astype(BF16)
        scratch[mv + 8 : 2 * mv + 16, :] = ins[i][pl.ds(base, mv + 8), :]
        outs[2 * i + 1][...] = shifted_rows(scratch, live + 8 - base, mv).astype(BF16)


def edges(tab, arrays, n, mv):
    slot, width = arrays[0].shape
    block = min(width, 1024)
    count = len(arrays)
    return pl.pallas_call(
        functools.partial(edges_kernel, n, mv, count),
        out_shape=[jax.ShapeDtypeStruct((mv, width), BF16)] * (2 * count),
        grid=(width // block,),
        in_specs=[SMEM] + [pl.BlockSpec((slot, block), lambda i: (0, i))] * count,
        out_specs=[pl.BlockSpec((mv, block), lambda i: (0, i))] * (2 * count),
        scratch_shapes=[pltpu.VMEM((2 * mv + 32, block), F32)],
        compiler_params=params(),
        cost_estimate=cost(0, count * slot * width * 5),
    )(tab, *arrays)


def weights_kernel(n, tab, own, left, right, out, src, dst):
    slot, mv = own.shape[0], left.shape[0]
    relayout(tab, n, own[...], left[...], right[...], src, dst)
    start, end = new_range(tab, n, tab[3 * n + 1])
    row = lax.broadcasted_iota(jnp.int32, own.shape, 0)
    kept = jnp.where(row < end - start, dst[mv : mv + slot, :], 0.0).astype(BF16)
    if out.shape[0] > slot:
        kept = jnp.concatenate([kept, jnp.zeros((out.shape[0] - slot, kept.shape[1]), BF16)])
    out[...] = kept


def new_weights(tab, own, left, right, n, rows):
    slot, width = own.shape
    mv = left.shape[0]
    block = min(width, 512)
    return pl.pallas_call(
        functools.partial(weights_kernel, n),
        out_shape=jax.ShapeDtypeStruct((rows, width), BF16),
        grid=(width // block,),
        in_specs=[SMEM, pl.BlockSpec((slot, block), lambda i: (0, i))]
        + [pl.BlockSpec((mv, block), lambda i: (0, i))] * 2,
        out_specs=pl.BlockSpec((rows, block), lambda i: (0, i)),
        scratch_shapes=[
            pltpu.VMEM((2 * slot + mv + 8, block), F32),
            pltpu.VMEM((slot + 2 * mv + 8, block), F32),
        ],
        compiler_params=params(),
        cost_estimate=cost(0, slot * width * 8),
    )(tab, own, left, right)


def forward_kernel(sent, tab, *refs):
    pieces, (mine, other, send, keep, hid) = refs[:-5], refs[-5:]
    rows, tokens = pieces[0].shape[1:]

    @pl.when(pl.program_id(0) == 0)
    def _():
        for i, piece in enumerate(pieces):
            for e in range(2):
                hid[i * tokens : (i + 1) * tokens, e * rows : (e + 1) * rows] = (
                    piece[e].astype(F32).T.astype(BF16)
                )

    for i in range(len(pieces)):
        block = hid[i * tokens : (i + 1) * tokens, :]
        part = jnp.dot(block[:, :rows], mine[...], preferred_element_type=F32)
        part = part + jnp.dot(block[:, rows:], other[...], preferred_element_type=F32)
        if i < sent:
            send[i, 0] = part.astype(BF16)
        else:
            keep[i - sent, 0] = part.astype(BF16)


def forward_half(tab, pieces, mine, other, sent, n, n_dp, half):
    rows, tokens = pieces[0].shape[1:]
    width = mine.shape[1]
    block = width // (2 * n_dp)
    count = len(pieces)

    def columns(s, tab):
        return 0, lax.rem(tab[3 * n + 2] + s, n_dp) * 2 + half

    def whole(s, tab):
        return 0, 0, 0

    def out_block(s, tab):
        return 0, s, 0, 0

    return pl.pallas_call(
        functools.partial(forward_kernel, sent),
        out_shape=[
            jax.ShapeDtypeStruct((sent, n_dp, tokens, block), BF16),
            jax.ShapeDtypeStruct((count - sent, n_dp, tokens, block), BF16),
        ],
        grid_spec=pltpu.PrefetchScalarGridSpec(
            num_scalar_prefetch=1,
            grid=(n_dp,),
            in_specs=[pl.BlockSpec((2, rows, tokens), whole)] * count
            + [pl.BlockSpec((rows, block), columns)] * 2,
            out_specs=[
                pl.BlockSpec((sent, 1, tokens, block), out_block),
                pl.BlockSpec((count - sent, 1, tokens, block), out_block),
            ],
            scratch_shapes=[pltpu.VMEM((count * tokens, 2 * rows), BF16)],
        ),
        compiler_params=params(),
        cost_estimate=cost(2 * count * tokens * 2 * rows * width // 2, 15e6),
    )(tab, *pieces, mine, other)


def adam_kernel(n, pieces, grads, scale, tab, *refs):
    ht_refs, refs = refs[: pieces + 1], refs[pieces + 1 :]
    og_refs, refs = refs[:grads], refs[grads:]
    own, left, right, outs = refs[0:3], refs[3:6], refs[6:9], refs[9:12]
    src, ht, og, moved = refs[12], refs[13], refs[14], refs[15:18]
    slot, mv = own[0].shape[0], left[0].shape[0]
    tokens = ht_refs[0].shape[2]

    @pl.when(pl.program_id(0) == 0)
    def _():
        for i in range(pieces):
            ht[:, i * tokens : (i + 1) * tokens] = ht_refs[i][0]
            ht[:, (pieces + i) * tokens : (pieces + i + 1) * tokens] = ht_refs[pieces][i]

    first = 0
    for ref in og_refs:
        og[first : first + ref.shape[0], :] = ref[...]
        first += ref.shape[0]
    for i in range(3):
        relayout(tab, n, own[i][...], left[i][...], right[i][...], src, moved[i])
    start, end = new_range(tab, n, tab[3 * n + 1])
    step = slot // 2 if slot % 16 == 0 else slot
    for base in range(0, slot, step):
        grad = jnp.dot(ht[base : base + step, :], og[...], preferred_element_type=F32) * scale
        rows = slice(mv + base, mv + base + step)
        master, first_old, second_old = (ref[rows, :] for ref in moved)
        first_next = 0.9 * first_old + 0.1 * grad
        second_next = 0.95 * second_old + 0.05 * grad * grad
        master_next = master - 0.001 * (first_next / (jnp.sqrt(second_next) + 1e-08) + 0.1 * master)
        live = lax.broadcasted_iota(jnp.int32, grad.shape, 0) + base < end - start
        for out, value in zip(outs, (master_next, first_next, second_next)):
            out[base : base + step, :] = jnp.where(live, value, 0.0)


def adam(tab, pieces, partner, grads, own, left, right, n, scale):
    rows, tokens = pieces[0].shape[1:]
    slot, width = own[0].shape
    mv = left[0].shape[0]
    block = min(width, 512)
    total = sum(g.shape[0] for g in grads)
    count = len(pieces)

    def column(i):
        return 0, i

    return pl.pallas_call(
        functools.partial(adam_kernel, n, count, len(grads), scale),
        out_shape=[jax.ShapeDtypeStruct((slot, width), F32)] * 3,
        grid=(width // block,),
        in_specs=[SMEM]
        + [pl.BlockSpec((1, rows, tokens), lambda i: (0, 0, 0))] * count
        + [pl.BlockSpec((count, rows, tokens), lambda i: (0, 0, 0))]
        + [pl.BlockSpec((g.shape[0], block), column) for g in grads]
        + [pl.BlockSpec((slot, block), column)] * 3
        + [pl.BlockSpec((mv, block), column)] * 6,
        out_specs=[pl.BlockSpec((slot, block), column)] * 3,
        scratch_shapes=[
            pltpu.VMEM((2 * slot + mv + 8, block), F32),
            pltpu.VMEM((rows, total), BF16),
            pltpu.VMEM((total, block), BF16),
        ]
        + [pltpu.VMEM((slot + 2 * mv + 8, block), F32)] * 3,
        compiler_params=params(),
        cost_estimate=cost(2 * total * slot * width, 95e6),
    )(tab, *pieces, partner, *grads, *own, *left, *right)


def swap(value, mask):
    n = lax.axis_size("fsdp")
    return lax.ppermute(value, "fsdp", [(i, i ^ mask) for i in range(n)])


def along(value, steps):
    n = lax.axis_size("fsdp")
    return lax.ppermute(value, "fsdp", [(i, i + steps) for i in range(n) if 0 <= i + steps < n])


def turn(value, steps):
    n = lax.axis_size("dp")
    return lax.ppermute(value, "dp", [(i, (i + steps) % n) for i in range(n)])


def gathered(value, groups):
    if groups != 4:
        return [value] + [swap(value, 2 * rel) for rel in range(1, groups)]
    half = value.shape[0] // 2
    x, y = swap(value, 2), swap(value, 4)
    return [value, x, y, swap(y[:half], 2), swap(x[half:], 4)]


def local(gate, up, out_grad, master_old, moment1_old, moment2_old, old_bounds, new_bounds, rank_map):
    n, n_dp = lax.axis_size("fsdp"), lax.axis_size("dp")
    groups = n // 2
    tokens, block_rows = gate.shape
    slot, width = master_old.shape[1:]
    rows = round_up(slot, 16)
    mv = round_up((block_rows // n + 1) // 2, 16)
    scale = 1.0 / math.sqrt(tokens * n)
    index = jnp.stack([lax.axis_index("fsdp"), lax.axis_index("dp")]).astype(jnp.int32)
    tab = jnp.concatenate([old_bounds[0], new_bounds[0], rank_map[0], index])
    own = [master_old[0], moment1_old[0], moment2_old[0]]

    first, last = edges(tab, own[:1], n, mv)
    master_right, master_left = along(first, -1), along(last, 1)
    windows = hidden_windows(tab, gate, up, n, rows)
    pieces = [windows[0]] + [swap(windows[rel], 2 * rel) for rel in range(1, groups)]
    first1, last1, first2, last2 = edges(tab, own[1:], n, mv)
    right = [master_right, along(first1, -1), along(first2, -1)]
    left = [master_left, along(last1, 1), along(last2, 1)]

    mine = new_weights(tab, own[0], left[0], right[0], n, rows)
    other = swap(mine, 1)
    halves = []
    for half in range(2):
        if groups == 4:
            near, far = (1, 2) if half == 0 else (2, 1)
            order = [pieces[near], pieces[3], pieces[0], pieces[far]]
            send, keep = forward_half(tab, order, mine, other, 2, n, n_dp, half)
            came = swap(send, 2 * near)
            passed = (keep[1].astype(F32) + came[1].astype(F32)).astype(BF16)
            total = keep[0].astype(F32) + came[0].astype(F32) + swap(passed, 2 * far).astype(F32)
        else:
            order = pieces[1:] + pieces[:1]
            send, keep = forward_half(tab, order, mine, other, groups - 1, n, n_dp, half)
            total = keep[0].astype(F32)
            for rel in range(1, groups):
                total = total + swap(send[rel - 1], 2 * rel).astype(F32)
        low = total.astype(BF16)
        out = total[0]
        for steps in range(1, n_dp):
            out = out + turn(low[steps], steps).astype(F32)
        halves.append(out)
    mlp_out = jnp.concatenate(halves, axis=1)

    grads = gathered(out_grad, groups)
    grads = grads + [swap(g, 1) for g in grads]
    partner = swap(jnp.stack([piece[1] for piece in pieces]), 1)
    master, first_next, second_next = adam(tab, pieces, partner, grads, own, left, right, n, scale)
    return mlp_out, master[None], first_next[None], second_next[None]


def solution(mesh):
    placed = (
        P("fsdp", "dp"),
        P("fsdp", "dp"),
        P("fsdp", None),
        P("dp", "fsdp", None),
        P("dp", "fsdp", None),
        P("dp", "fsdp", None),
        P("dp", None),
        P("dp", None),
        P("dp", None),
    )
    return jax.shard_map(
        local,
        mesh=mesh,
        in_specs=placed,
        out_specs=(
            P("fsdp", "dp"),
            P("dp", "fsdp", None),
            P("dp", "fsdp", None),
            P("dp", "fsdp", None),
        ),
        check_vma=False,
    )
```

```python
import functools
import math

import jax
import jax.numpy as jnp
from jax import lax
from jax.experimental import pallas as pl
from jax.experimental.pallas import tpu as pltpu
from jax.sharding import PartitionSpec as P

BF16 = jnp.bfloat16
F32 = jnp.float32
VMEM_BYTES = 58 * 1024 * 1024
SMEM = pl.BlockSpec(memory_space=pltpu.SMEM)


def round_up(value, step):
    return -(-value // step) * step


def params():
    return pltpu.CompilerParams(vmem_limit_bytes=VMEM_BYTES)


def cost():
    return pl.CostEstimate(flops=1, bytes_accessed=1, transcendentals=0)


def old_range(tab, n, q):
    return tab[q], tab[q + 1]


def new_range(tab, n, q):
    k = tab[2 * n + 1 + q]
    return tab[n + 1 + jnp.minimum(k, n - 1)], tab[n + 1 + jnp.minimum(k + 1, n - 1)]


def shifted_rows(ref, start, rows):
    base = pl.multiple_of((start // 8) * 8, 8)
    rem = start - base
    x = ref[pl.ds(base, rows + 8), :]
    lanes = x.shape[1]
    y = pltpu.roll(x.reshape(rows // 8 + 1, 8, lanes), (8 - rem) % 8, 1)
    sublane = lax.broadcasted_iota(jnp.int32, (rows // 8, 8, lanes), 1)
    return jnp.where(sublane < 8 - rem, y[:-1], y[1:]).reshape(rows, lanes)


def place_groups(y, rem):
    before = jnp.concatenate([y[:1], y])
    here = jnp.concatenate([y, y[-1:]])
    sublane = lax.broadcasted_iota(jnp.int32, (1, 8, y.shape[2]), 1)
    return jnp.where(sublane < rem, before, here)


def rolled(x, rem):
    return pltpu.roll(x.reshape(x.shape[0] // 8, 8, x.shape[1]), rem, 1)


def relayout(tab, n, own, inner, outer, dst):
    slot, mv = own.shape[0], inner.shape[0]
    lanes = own.shape[1]
    q = tab[3 * n + 1]
    odd = lax.rem(q, 2) == 1
    old_start, old_end = old_range(tab, n, q)
    new_start, _ = new_range(tab, n, q)
    start = slot + jnp.clip(old_start - new_start, -slot, mv)
    base = pl.multiple_of((start // 8) * 8, 8)
    rem = start - base
    left = jnp.where(odd, inner, outer).astype(F32)
    y = jnp.concatenate([rolled(left, rem), rolled(own, rem)])
    dst[pl.ds(base, mv + slot + 8), :] = place_groups(y, rem).reshape(mv + slot + 8, lanes)
    start = mv + slot + jnp.clip(old_end - new_start, -mv, slot)
    base = pl.multiple_of((start // 8) * 8, 8)
    rem = start - base
    right = place_groups(rolled(jnp.where(odd, outer, inner).astype(F32), rem), rem).reshape(mv + 8, lanes)
    row = lax.broadcasted_iota(jnp.int32, (mv + 8, lanes), 0)
    dst[pl.ds(base, mv + 8), :] = jnp.where(row >= rem, right, dst[pl.ds(base, mv + 8), :])


def relayout_rows(slot, mv):
    return 2 * slot + 2 * mv + 16


def hidden_kernel(n, rows, tab, gate, up, *refs):
    outs, scratch = refs[:-1], refs[-1]
    tokens, width = gate.shape
    for first in range(0, width, 128):
        last = min(first + 128, width)
        g = gate[:, first:last].astype(F32)
        h = g / (1.0 + jnp.exp(-g)) * up[:, first:last].astype(F32)
        scratch[first:last, :] = h.T
    scratch[width:, :] = jnp.zeros((scratch.shape[0] - width, tokens), F32)
    q = tab[3 * n + 1]
    for rel, out in enumerate(outs):
        for other in range(2):
            start, _ = new_range(tab, n, q ^ (2 * rel + other))
            out[other] = shifted_rows(scratch, start, rows).astype(BF16)


def hidden_windows(tab, gate, up, n, rows):
    tokens, width = gate.shape
    shape = jax.ShapeDtypeStruct((2, rows, tokens), BF16)
    return pl.pallas_call(
        functools.partial(hidden_kernel, n, rows),
        out_shape=[shape] * (n // 2),
        in_specs=[SMEM, pl.BlockSpec(memory_space=pltpu.VMEM), pl.BlockSpec(memory_space=pltpu.VMEM)],
        out_specs=[pl.BlockSpec(memory_space=pltpu.VMEM)] * (n // 2),
        scratch_shapes=[pltpu.VMEM((round_up(width, 8) + rows + 8, tokens), F32)],
        compiler_params=params(),
        cost_estimate=cost(),
    )(tab, gate, up)


def edges_kernel(n, mv, count, block, starts, tab, *refs):
    ins, inner, outers, (head, tail, sems) = refs[:count], refs[count], refs[count + 1 : -3], refs[-3:]
    q = tab[3 * n + 1]
    odd = lax.rem(q, 2) == 1
    old_start, old_end = old_range(tab, n, q)
    live = old_end - old_start
    slot, width = ins[0].shape
    base = pl.multiple_of((jnp.clip(live - mv, 0, slot - mv - 8) // 8) * 8, 8)
    copies = []
    for i in range(count):
        copies.append(pltpu.make_async_copy(ins[i].at[pl.ds(0, mv)], head.at[i], sems.at[i, 0]))
        copies.append(
            pltpu.make_async_copy(ins[i].at[pl.ds(base, mv + 8)], tail.at[i, pl.ds(mv + 8, mv + 8)], sems.at[i, 1])
        )
    for copy in copies:
        copy.start()
    size = len(starts[0]) * count * block
    for i in range(count):
        copies[2 * i].wait()
        copies[2 * i + 1].wait()
        for part, blocks in enumerate(starts):
            for at, start in enumerate(blocks):
                columns = slice(start, start + block)
                first = head[i, :, columns].astype(BF16)
                last = shifted_rows(tail.at[i, :, columns], live + 8 - base, mv).astype(BF16)
                place = (at * count + i) * block
                outers[part][:, place : place + block] = jnp.where(odd, last, first)
                place += part * size
                inner[:, place : place + block] = jnp.where(odd, first, last)


def edges(tab, arrays, n, mv, block, starts):
    width = arrays[0].shape[1]
    count = len(arrays)
    return pl.pallas_call(
        functools.partial(edges_kernel, n, mv, count, block, starts),
        out_shape=[jax.ShapeDtypeStruct((mv, count * width), BF16)]
        + [jax.ShapeDtypeStruct((mv, count * width // len(starts)), BF16)] * len(starts),
        in_specs=[SMEM] + [pl.BlockSpec(memory_space=pl.ANY)] * count,
        out_specs=[pl.BlockSpec(memory_space=pltpu.VMEM)] * (1 + len(starts)),
        scratch_shapes=[
            pltpu.VMEM((count, mv, width), F32),
            pltpu.VMEM((count, 2 * mv + 32, width), F32),
            pltpu.SemaphoreType.DMA((count, 2)),
        ],
        compiler_params=params(),
        cost_estimate=cost(),
    )(tab, *arrays)


def weights_kernel(n, tab, own, inner, outer, out, dst):
    slot, mv = own.shape[0], inner.shape[0]
    relayout(tab, n, own[...], inner[...], outer[...], dst)
    start, end = new_range(tab, n, tab[3 * n + 1])
    row = lax.broadcasted_iota(jnp.int32, own.shape, 0)
    kept = jnp.where(row < end - start, dst[mv + slot : mv + 2 * slot, :], 0.0).astype(BF16)
    if out.shape[1] > slot:
        kept = jnp.concatenate([kept, jnp.zeros((out.shape[1] - slot, kept.shape[1]), BF16)])
    block = out.shape[2]
    for i in range(out.shape[0]):
        out[i] = kept[:, i * block : (i + 1) * block]


def new_weights(tab, own, inner, outer, n, n_dp, rows, half):
    slot, width = own.shape
    mv = inner.shape[0]
    block = width // (2 * n_dp)

    def group(s, tab):
        return lax.rem(tab[3 * n + 2] + s, n_dp)

    return pl.pallas_call(
        functools.partial(weights_kernel, n),
        out_shape=jax.ShapeDtypeStruct((2, rows, width // 4), BF16),
        grid_spec=pltpu.PrefetchScalarGridSpec(
            num_scalar_prefetch=1,
            grid=(n_dp,),
            in_specs=[
                pl.BlockSpec((slot, block), lambda s, tab: (0, 2 * group(s, tab) + half)),
                pl.BlockSpec((mv, block), lambda s, tab: (0, half * n_dp + group(s, tab))),
                pl.BlockSpec((mv, block), lambda s, tab: (0, group(s, tab))),
            ],
            out_specs=pl.BlockSpec((2, rows, block // 2), lambda s, tab: (0, 0, s)),
            scratch_shapes=[pltpu.VMEM((relayout_rows(slot, mv), block), F32)],
        ),
        compiler_params=params(),
        cost_estimate=cost(),
    )(tab, own, inner, outer)


def turned_kernel(piece, out):
    rows = piece.shape[1]
    for e in range(2):
        out[:, e * rows : (e + 1) * rows] = piece[e].astype(F32).T.astype(BF16)


def turned(piece):
    return pl.pallas_call(
        turned_kernel,
        out_shape=jax.ShapeDtypeStruct((piece.shape[2], 2 * piece.shape[1]), BF16),
        in_specs=[pl.BlockSpec(memory_space=pltpu.VMEM)],
        out_specs=pl.BlockSpec(memory_space=pltpu.VMEM),
        compiler_params=params(),
        cost_estimate=cost(),
    )(piece)


def forward_kernel(sent, tab, *refs):
    pieces, (mine, other, send, keep, hid, weights) = refs[:-6], refs[-6:]
    rows = mine.shape[1]
    tokens = send.shape[2]

    @pl.when(pl.program_id(0) == 0)
    def _():
        for i, piece in enumerate(pieces):
            hid[i * tokens : (i + 1) * tokens, :] = piece[...]

    weights[:rows, :] = mine[0]
    weights[rows:, :] = other[0]
    part = jnp.dot(hid[...], weights[...], preferred_element_type=F32).astype(BF16)
    for i in range(len(pieces)):
        block = part[i * tokens : (i + 1) * tokens, :]
        if i < sent:
            send[i, 0] = block
        else:
            keep[i - sent, 0] = block


def forward_chunk(tab, pieces, mine, other, sent, n_dp, at):
    tokens = pieces[0].shape[0]
    rows = mine.shape[1]
    block = mine.shape[2] // n_dp
    kept = len(pieces) - sent

    def out_block(s):
        return 0, s, 0, 0

    return pl.pallas_call(
        functools.partial(forward_kernel, sent),
        out_shape=[
            jax.ShapeDtypeStruct((sent, n_dp, tokens, block), BF16),
            jax.ShapeDtypeStruct((kept, n_dp, tokens, block), BF16),
        ],
        grid=(n_dp,),
        in_specs=[SMEM]
        + [pl.BlockSpec(pieces[0].shape, lambda s: (0, 0))] * len(pieces)
        + [pl.BlockSpec((1, rows, block), lambda s: (at, 0, s))] * 2,
        out_specs=[
            pl.BlockSpec((sent, 1, tokens, block), out_block),
            pl.BlockSpec((kept, 1, tokens, block), out_block),
        ],
        scratch_shapes=[
            pltpu.VMEM((len(pieces) * tokens, 2 * rows), BF16),
            pltpu.VMEM((2 * rows, block), BF16),
        ],
        compiler_params=params(),
        cost_estimate=cost(),
    )(tab, *pieces, mine, other)


def fill_tokens(ht_refs, ht):
    tokens = ht_refs[0].shape[2]
    for i, ref in enumerate(ht_refs):
        ht[:, i * tokens : (i + 1) * tokens] = ref[0]


def fill_grads(parity, og_refs, places, og):
    for ref, (at, flip, count, *more) in zip(og_refs, places):
        rows = ref.shape[0]
        if flip is None:
            og[at : at + rows, :] = ref[...]
        else:
            shift = (parity if flip == 0 else 1 - parity) * count + more[0]
            og[pl.ds(pl.multiple_of(at + shift, rows), rows), :] = ref[...]


def partner_kernel(n, pieces, places, tab, *refs):
    ht_refs, og_refs, (out, ht, og) = refs[:pieces], refs[pieces:-3], refs[-3:]

    @pl.when(pl.program_id(0) == 0)
    def _():
        fill_tokens(ht_refs, ht)

    fill_grads(lax.rem(tab[3 * n + 2], 2), og_refs, places, og)
    out[...] = jnp.dot(ht[...], og[...], preferred_element_type=F32).astype(BF16)


def partner_grad(tab, pieces, grads, places, n, part, parts):
    rows, tokens = pieces[0].shape[1:]
    width = grads[0].shape[1]
    block = min(width // parts, 512)
    steps = width // parts // block
    total = sum(g.shape[0] for g in grads)
    return pl.pallas_call(
        functools.partial(partner_kernel, n, len(pieces), places),
        out_shape=jax.ShapeDtypeStruct((rows, width // parts), BF16),
        grid=(steps,),
        in_specs=[SMEM]
        + [pl.BlockSpec((1, rows, tokens), lambda i: (1, 0, 0))] * len(pieces)
        + [pl.BlockSpec((g.shape[0], block), lambda i: (0, part * steps + i)) for g in grads],
        out_specs=pl.BlockSpec((rows, block), lambda i: (0, i)),
        scratch_shapes=[pltpu.VMEM((rows, total), BF16), pltpu.VMEM((total, block), BF16)],
        compiler_params=params(),
        cost_estimate=cost(),
    )(tab, *pieces, *grads)


def adam_kernel(n, pieces, places, scale, aliased, relayed, tab, *refs):
    ht_refs, refs = refs[:pieces], refs[pieces:]
    og_refs, refs = refs[: len(places)], refs[len(places) :]
    rest, own, (inner0, inner1, outer0, outer1, inner_both, outer_both) = refs[0], refs[1:4], refs[4:10]
    refs = refs[10:]
    relay, refs = refs[:relayed], refs[relayed + aliased :]
    outs, ht, og, moved = refs[0:3], refs[3], refs[4], refs[5:8]
    slot, mv = own[0].shape[0], inner0.shape[0]
    block = og.shape[1]
    even = lax.rem(pl.program_id(0), 2) == 0

    @pl.when(pl.program_id(0) == 0)
    def _():
        fill_tokens(ht_refs, ht)

    fill_grads(lax.rem(tab[3 * n + 2], 2), og_refs, places, og)
    inner = jnp.where(even, inner0[...], inner1[...])
    outer = jnp.where(even, outer0[...], outer1[...])
    relayout(tab, n, own[0][...], inner, outer, moved[0])
    for i in range(2):
        columns = slice(i * block, (i + 1) * block)
        outer = outer_both[:, columns]
        for ref in relay:
            outer = outer + ref[:, columns]
        relayout(tab, n, own[i + 1][...], inner_both[:, columns], outer, moved[i + 1])
    start, end = new_range(tab, n, tab[3 * n + 1])
    step = slot // 2 if slot % 16 == 0 else slot
    for base in range(0, slot, step):
        grad = jnp.dot(ht[base : base + step, :], og[...], preferred_element_type=F32)
        grad = (grad + rest[base : base + step, :].astype(F32)) * scale
        rows = slice(mv + slot + base, mv + slot + base + step)
        master, first_old, second_old = (ref[rows, :] for ref in moved)
        first_next = 0.9 * first_old + 0.1 * grad
        second_next = 0.95 * second_old + 0.05 * grad * grad
        master_next = master - 0.001 * (first_next / (jnp.sqrt(second_next) + 1e-08) + 0.1 * master)
        live = lax.broadcasted_iota(jnp.int32, grad.shape, 0) + base < end - start
        for out, value in zip(outs, (master_next, first_next, second_next)):
            out[base : base + step, :] = jnp.where(live, value, 0.0)


def adam_part(tab, pieces, grads, places, rest, own, edge, both, outs, n, n_dp, scale, part, parts):
    rows, tokens = pieces[0].shape[1:]
    slot, width = own[0].shape
    mv = both[0].shape[0]
    block = width // (2 * n_dp)
    steps = width // parts // block
    total = sum(g.shape[0] for g in grads)
    inner, outers = edge
    split = parts // (width // rest.shape[1])

    def column(i):
        return 0, part * steps + i

    def first(i):
        return 0, (part * steps + i) // 2

    def second(i):
        return 0, n_dp + (part * steps + i) // 2

    def inner_both(i):
        return 0, part * steps + i

    operands = [tab, *pieces, *grads, rest, *own, inner, inner, *outers, *both, *outs]
    return pl.pallas_call(
        functools.partial(adam_kernel, n, len(pieces), places, scale, len(outs), len(both) - 2),
        out_shape=[jax.ShapeDtypeStruct((slot, width), F32)] * 3,
        grid=(steps,),
        in_specs=[SMEM]
        + [pl.BlockSpec((1, rows, tokens), lambda i: (0, 0, 0))] * len(pieces)
        + [pl.BlockSpec((g.shape[0], block), column) for g in grads]
        + [pl.BlockSpec((rows, block), lambda i: (0, part % split * steps + i))]
        + [pl.BlockSpec((slot, block), column)] * 3
        + [pl.BlockSpec((mv, block), first), pl.BlockSpec((mv, block), second)]
        + [pl.BlockSpec((mv, block), first)] * 2
        + [pl.BlockSpec((mv, 2 * block), inner_both)]
        + [pl.BlockSpec((mv, 2 * block), lambda i: (0, i))] * (len(both) - 1)
        + [pl.BlockSpec(memory_space=pl.ANY)] * len(outs),
        out_specs=[pl.BlockSpec((slot, block), column)] * 3,
        scratch_shapes=[
            pltpu.VMEM((rows, total), BF16),
            pltpu.VMEM((total, block), BF16),
        ]
        + [pltpu.VMEM((relayout_rows(slot, mv), block), F32)] * 3,
        input_output_aliases={len(operands) - 3 + i: i for i in range(3)} if outs else {},
        compiler_params=params(),
        cost_estimate=cost(),
    )(*operands)


def swap(value, mask):
    n = lax.axis_size("fsdp")
    return lax.ppermute(value, "fsdp", [(i, i ^ mask) for i in range(n)])


def swap_outer(value, middle=True):
    n = lax.axis_size("fsdp")
    pairs = [(i, i + 1 if i % 2 else i - 1) for i in range(1, n - 1)]
    return lax.ppermute(value, "fsdp", [(i, j) for i, j in pairs if middle or {i, j} != {3, 4}])


def relay_first(value):
    return lax.ppermute(value, "fsdp", [(3, 7), (4, 0)])


def relay_second(value):
    return lax.ppermute(value, "fsdp", [(7, 4), (0, 3)])


def turn(value, steps):
    n = lax.axis_size("dp")
    return lax.ppermute(value, "dp", [(i, (i + steps) % n) for i in range(n)])


def stage(*values):
    return lax.optimization_barrier(values)


def add(a, b):
    return (a.astype(F32) + b.astype(F32)).astype(BF16)


def local(gate, up, out_grad, master_old, moment1_old, moment2_old, old_bounds, new_bounds, rank_map):
    n, n_dp = lax.axis_size("fsdp"), lax.axis_size("dp")
    groups = n // 2
    square = groups == 4
    chunks, parts = 4, 4
    tokens, block_rows = gate.shape
    slot, width = master_old.shape[1:]
    rows = round_up(slot, 16)
    mv = round_up((block_rows // n + 1) // 2, 16)
    scale = 1.0 / math.sqrt(tokens * n)
    index = jnp.stack([lax.axis_index("fsdp"), lax.axis_index("dp")]).astype(jnp.int32)
    tab = jnp.concatenate([old_bounds[0], new_bounds[0], rank_map[0], index])
    own = [master_old[0], moment1_old[0], moment2_old[0]]
    half = tokens // 2
    parity = lax.rem(lax.axis_index("dp"), 2)
    mine_grad = lax.dynamic_slice_in_dim(out_grad, parity * half, half, 0)

    block = width // (2 * n_dp)
    steps = width // parts // block
    halves = 2
    order = [2, 3, 0, 1] if square else list(range(1, groups)) + [0]
    sent = 2 if square else groups - 1

    def flip(value):
        return lax.ppermute(value, "dp", [(i, i ^ 1) for i in range(n_dp)])

    def forward(chunk):
        mine, other = weights[chunk // 2]
        return forward_chunk(tab, [tokens_first[i] for i in order], mine, other, sent, n_dp, chunk % 2)

    def first_sum(chunk):
        send = sends[chunk]
        if square:
            return [swap(send, 4)]
        return [swap(send[rel - 1], 2 * rel) for rel in range(1, groups)]

    def second_sum(chunk):
        total = keeps[chunk][0].astype(F32)
        if square:
            passed = swap(add(keeps[chunk][1], came[chunk][0][1]), 2)
            return total + came[chunk][0][0].astype(F32) + passed.astype(F32)
        for value in came[chunk]:
            total = total + value.astype(F32)
        return total

    def over_dp(chunk):
        low = totals[chunk].astype(BF16)
        out = totals[chunk][0]
        for turned_by in range(1, n_dp):
            out = out + turn(low[turned_by], turned_by).astype(F32)
        return out

    def step(part, outs):
        moved = (moving_inner, *moved_outer[part])
        value = partner[part // (parts // halves)]
        return list(
            adam_part(tab, pieces, grads, places, value, own, (inner, outers), moved, outs, n, n_dp, scale, part, parts)
        )

    inner, *outers = edges(
        tab, own[:1], n, mv, block, [[(2 * j + h) * block for j in range(n_dp)] for h in range(2)]
    )
    tab, inner, outers, mine_grad = stage(tab, inner, outers, mine_grad)
    outers = list(outers)
    inner, outers[0] = swap(inner, 1), swap_outer(outers[0])
    windows = list(hidden_windows(tab, gate, up, n, rows))
    moving = list(
        edges(
            tab,
            own[1:],
            n,
            mv,
            block,
            [[(part * steps + i) * block for i in range(steps)] for part in range(parts)],
        )
    )
    quarter = half // 2
    grad_y = [swap(mine_grad[:quarter], 4)] if square else []
    tab, inner, outers, mine_grad, grad_y, windows, moving = stage(
        tab, inner, outers, mine_grad, grad_y, windows, moving
    )

    outers, moving, grad_y = list(outers), list(moving), list(grad_y)
    outers[1] = swap_outer(outers[1])
    flips_y = []
    if square:
        grad_y.append(swap(mine_grad[quarter:], 4))
        flips_y.append(flip(grad_y[0]))
    moving_inner = swap(moving[0], 1)
    mine = new_weights(tab, own[0], inner, outers[0], n, n_dp, rows, 0)
    tab, outers, mine_grad, grad_y, flips_y, windows, moving, moving_inner, mine = stage(
        tab, outers, mine_grad, grad_y, flips_y, windows, moving, moving_inner, mine
    )

    pieces, flips_y = list(windows), list(flips_y)
    for rel in range(1, groups):
        pieces[rel] = swap(pieces[rel], 2 * rel)
    weights = [(mine, swap(mine, 1))]
    if square:
        flips_y.append(flip(grad_y[1]))
    mine = new_weights(tab, own[0], inner, outers[1], n, n_dp, rows, 1)
    tokens_first = [turned(pieces[0])]
    tab, mine_grad, flips_y, moving, pieces, weights, mine, tokens_first = stage(
        tab, mine_grad, flips_y, moving, pieces, weights, mine, tokens_first
    )

    weights = list(weights) + [(mine, swap(mine, 1))]
    tokens_first = list(tokens_first) + [turned(piece) for piece in pieces[1:]]
    sends, keeps, came, totals = [None] * chunks, [None] * chunks, [None] * chunks, [None] * chunks
    sends[0], keeps[0] = forward(0)
    grad_x = swap(mine_grad, 2) if square else mine_grad
    relays = [relay_first(moving[2]), relay_first(moving[4])] if square else []
    tab, grad_x, moving, weights, sends, keeps, tokens_first, relays = stage(
        tab, grad_x, moving, weights, sends, keeps, tokens_first, relays
    )

    sends, keeps, relays = list(sends), list(keeps), list(relays)
    moved_outer = [(swap_outer(moving[1]),)]
    if square:
        relays[0] = relay_second(relays[0])
        grad_g, flip_x = swap(grad_x, 4), flip(grad_x)
    else:
        grad_g, flip_x = grad_x, grad_x
    sends[1], keeps[1] = forward(1)
    tab, grad_x, grad_g, flip_x, moving, moved_outer, sends, keeps, relays = stage(
        tab, grad_x, grad_g, flip_x, moving, moved_outer, sends, keeps, relays
    )

    sends, keeps, moved_outer = list(sends), list(keeps), list(moved_outer)
    moved_outer.append((swap_outer(moving[2], not square), *relays[:1]))
    came[0] = first_sum(0)
    flip_g = flip(grad_g) if square else grad_g
    sends[2], keeps[2] = forward(2)
    sends[3], keeps[3] = forward(3)
    tab, flip_g, moving, moved_outer, sends, keeps, came, relays = stage(
        tab, flip_g, moving, moved_outer, sends, keeps, came, relays
    )

    keeps, came, moved_outer, relays = list(keeps), list(came), list(moved_outer), list(relays)
    if square:
        grads = [out_grad, grad_x, *grad_y, grad_g, flip_x, *flips_y, flip_g]
        places = [(0, None, tokens)]
        for which in range(2):
            places += [(tokens, which, half, 0), (2 * tokens, which, half, 0), (2 * tokens, which, half, quarter)]
            places += [(3 * tokens, which, half, 0)]
    else:
        grads = [out_grad] + [swap(out_grad, 2 * rel) for rel in range(1, groups)]
        places = [(i * tokens, None, tokens) for i in range(groups)]
    moved_outer.append((swap_outer(moving[3]),))
    if square:
        relays[1] = relay_second(relays[1])
    came[1] = first_sum(1)
    totals[0] = second_sum(0)
    partner = [partner_grad(tab, pieces, grads, places, n, i, halves) for i in range(halves)]
    tab, moving, moved_outer, sends, came, totals, partner, relays = stage(
        tab, moving, moved_outer, sends, came, totals, partner, relays
    )

    came, totals, moved_outer = list(came), list(totals), list(moved_outer)
    moved_outer.append((swap_outer(moving[4], not square), *relays[1:]))
    came[2] = first_sum(2)
    totals[1] = second_sum(1)
    partner = [swap(value, 1) for value in partner]
    outs = step(1, step(0, []))
    tab, moved_outer, sends, came, totals, partner, outs = stage(
        tab, moved_outer, sends, came, totals, partner, outs
    )

    came, totals = list(came), list(totals)
    came[3] = first_sum(3)
    totals[2] = second_sum(2)
    results = [over_dp(0), over_dp(1)]
    outs = step(3, step(2, list(outs)))
    tab, came, totals, outs = stage(tab, came, totals, list(outs))

    totals = list(totals)
    totals[3] = second_sum(3)
    results.append(over_dp(2))
    results.append(over_dp(3))
    mlp_out = jnp.concatenate(results, axis=1)
    return mlp_out, outs[0][None], outs[1][None], outs[2][None]


def solution(mesh):
    placed = (
        P("fsdp", "dp"),
        P("fsdp", "dp"),
        P("fsdp", None),
        P("dp", "fsdp", None),
        P("dp", "fsdp", None),
        P("dp", "fsdp", None),
        P("dp", None),
        P("dp", None),
        P("dp", None),
    )
    return jax.shard_map(
        local,
        mesh=mesh,
        in_specs=placed,
        out_specs=(
            P("fsdp", "dp"),
            P("dp", "fsdp", None),
            P("dp", "fsdp", None),
            P("dp", "fsdp", None),
        ),
        check_vma=False,
    )
```

```python
import functools
import math

import jax
import jax.numpy as jnp
from jax import lax
from jax.experimental import pallas as pl
from jax.experimental.pallas import tpu as pltpu
from jax.sharding import PartitionSpec as P

BF16 = jnp.bfloat16
F32 = jnp.float32
VMEM_BYTES = 58 * 1024 * 1024
SMEM = pl.BlockSpec(memory_space=pltpu.SMEM)


def round_up(value, step):
    return -(-value // step) * step


def params():
    return pltpu.CompilerParams(vmem_limit_bytes=VMEM_BYTES)


def cost():
    return pl.CostEstimate(flops=1, bytes_accessed=1, transcendentals=0)


def old_range(tab, n, q):
    return tab[q], tab[q + 1]


def new_range(tab, n, q):
    k = tab[2 * n + 1 + q]
    return tab[n + 1 + jnp.minimum(k, n - 1)], tab[n + 1 + jnp.minimum(k + 1, n - 1)]


def shifted_rows(ref, start, rows):
    base = pl.multiple_of((start // 8) * 8, 8)
    rem = start - base
    x = ref[pl.ds(base, rows + 8), :]
    lanes = x.shape[1]
    y = pltpu.roll(x.reshape(rows // 8 + 1, 8, lanes), (8 - rem) % 8, 1)
    sublane = lax.broadcasted_iota(jnp.int32, (rows // 8, 8, lanes), 1)
    return jnp.where(sublane < 8 - rem, y[:-1], y[1:]).reshape(rows, lanes)


def piece_rows(rows, sizes=(48, 32, 24, 16, 8)):
    return next(size for size in sizes if rows % size == 0)


def rolled(x, rem):
    return pltpu.roll(x.reshape(x.shape[0] // 8, 8, x.shape[1]), rem, 1)


def place_rows(parts, dst, start, keep):
    base = pl.multiple_of((start // 8) * 8, 8)
    rem = start - base
    last = None
    at = 0
    for load, rows in parts:
        size = piece_rows(rows)
        for first in range(0, rows, size):
            y = rolled(load(first, size), rem)
            lanes = y.shape[2]
            if last is None:
                last = dst[pl.ds(base, 8), :].reshape(1, 8, lanes) if keep else y[:1]
            before = jnp.concatenate([last, y[:-1]]) if size > 8 else last
            sublane = lax.broadcasted_iota(jnp.int32, y.shape, 1)
            out = jnp.where(sublane < rem, before, y)
            dst[pl.ds(pl.multiple_of(base + at, 8), size), :] = out.reshape(size, lanes)
            last = y[-1:]
            at += size
    dst[pl.ds(pl.multiple_of(base + at, 8), 8), :] = last.reshape(8, last.shape[2])


def relayout(tab, n, own, left, right, slot, mv, dst):
    q = tab[3 * n + 1]
    old_start, old_end = old_range(tab, n, q)
    new_start, _ = new_range(tab, n, q)
    start = slot + jnp.clip(old_start - new_start, -slot, mv)
    place_rows([(left, mv), (own, slot)], dst, start, False)
    start = mv + slot + jnp.clip(old_end - new_start, -mv, slot)
    place_rows([(right, mv)], dst, start, True)


def from_ref(ref, columns=slice(None)):
    return lambda first, rows: ref[first : first + rows, columns]


def chosen(flag, a, b):
    return lambda first, rows: jnp.where(flag, a(first, rows), b(first, rows)).astype(F32)


def relayout_rows(slot, mv):
    return 2 * slot + 2 * mv + 32


def hidden_kernel(n, rows, tab, gate, up, *refs):
    outs, scratch = refs[:-1], refs[-1]
    tokens, width = gate.shape
    for first in range(0, width, 128):
        last = min(first + 128, width)
        g = gate[:, first:last].astype(F32)
        h = g / (1.0 + jnp.exp(-g)) * up[:, first:last].astype(F32)
        scratch[first:last, :] = h.T
    scratch[width:, :] = jnp.zeros((scratch.shape[0] - width, tokens), F32)
    q = tab[3 * n + 1]
    piece = piece_rows(rows, (48, 16))
    for rel, out in enumerate(outs):
        for other in range(2):
            start, _ = new_range(tab, n, q ^ (2 * rel + other))
            for row in range(0, rows, piece):
                out[other, row : row + piece, :] = shifted_rows(scratch, start + row, piece).astype(BF16)


def hidden_windows(tab, gate, up, n, rows):
    tokens, width = gate.shape
    shape = jax.ShapeDtypeStruct((2, rows, tokens), BF16)
    return pl.pallas_call(
        functools.partial(hidden_kernel, n, rows),
        out_shape=[shape] * (n // 2),
        in_specs=[SMEM, pl.BlockSpec(memory_space=pltpu.VMEM), pl.BlockSpec(memory_space=pltpu.VMEM)],
        out_specs=[pl.BlockSpec(memory_space=pltpu.VMEM)] * (n // 2),
        scratch_shapes=[pltpu.VMEM((round_up(width, 8) + rows + 8, tokens), F32)],
        compiler_params=params(),
        cost_estimate=cost(),
    )(tab, gate, up)


def edges_kernel(n, mv, count, block, starts, tab, *refs):
    ins, inner, outers, (head, tail, sems) = refs[:count], refs[count], refs[count + 1 : -3], refs[-3:]
    q = tab[3 * n + 1]
    odd = lax.rem(q, 2) == 1
    old_start, old_end = old_range(tab, n, q)
    live = old_end - old_start
    slot, width = ins[0].shape
    base = pl.multiple_of((jnp.clip(live - mv, 0, slot - mv - 8) // 8) * 8, 8)
    copies = []
    for i in range(count):
        copies.append(pltpu.make_async_copy(ins[i].at[pl.ds(0, mv)], head.at[i], sems.at[i, 0]))
        copies.append(
            pltpu.make_async_copy(ins[i].at[pl.ds(base, mv + 8)], tail.at[i, pl.ds(mv + 8, mv + 8)], sems.at[i, 1])
        )
    for copy in copies:
        copy.start()
    size = len(starts[0]) * count * block
    piece = piece_rows(mv, (48, 32, 16))
    for i in range(count):
        copies[2 * i].wait()
        copies[2 * i + 1].wait()
        for part, blocks in enumerate(starts):
            for at, start in enumerate(blocks):
                columns = slice(start, start + block)
                place = (at * count + i) * block
                for row in range(0, mv, piece):
                    rows = slice(row, row + piece)
                    first = head[i, rows, columns]
                    last = shifted_rows(tail.at[i, :, columns], live + 8 - base + row, piece)
                    outers[part][rows, place : place + block] = jnp.where(odd, last, first).astype(BF16)
                    inner_place = place + part * size
                    inner[rows, inner_place : inner_place + block] = jnp.where(odd, first, last).astype(BF16)


def edges(tab, arrays, n, mv, block, starts):
    width = arrays[0].shape[1]
    count = len(arrays)
    return pl.pallas_call(
        functools.partial(edges_kernel, n, mv, count, block, starts),
        out_shape=[jax.ShapeDtypeStruct((mv, count * width), BF16)]
        + [jax.ShapeDtypeStruct((mv, count * width // len(starts)), BF16)] * len(starts),
        in_specs=[SMEM] + [pl.BlockSpec(memory_space=pl.ANY)] * count,
        out_specs=[pl.BlockSpec(memory_space=pltpu.VMEM)] * (1 + len(starts)),
        scratch_shapes=[
            pltpu.VMEM((count, mv, width), F32),
            pltpu.VMEM((count, 2 * mv + 32, width), F32),
            pltpu.SemaphoreType.DMA((count, 2)),
        ],
        compiler_params=params(),
        cost_estimate=cost(),
    )(tab, *arrays)


def weights_kernel(n, tab, own, inner, outer, out, dst):
    slot, mv = own.shape[0], inner.shape[0]
    q = tab[3 * n + 1]
    odd = lax.rem(q, 2) == 1
    left = chosen(odd, from_ref(inner), from_ref(outer))
    right = chosen(odd, from_ref(outer), from_ref(inner))
    relayout(tab, n, from_ref(own), left, right, slot, mv, dst)
    start, end = new_range(tab, n, q)
    block = out.shape[2]
    size = piece_rows(out.shape[1], (48, 32, 16))
    for first in range(0, out.shape[1], size):
        kept = dst[mv + slot + first : mv + slot + first + size, :]
        row = lax.broadcasted_iota(jnp.int32, kept.shape, 0) + first
        kept = jnp.where(row < end - start, kept, 0.0).astype(BF16)
        for i in range(out.shape[0]):
            out[i, first : first + size, :] = kept[:, i * block : (i + 1) * block]


def new_weights(tab, own, inner, outer, n, n_dp, rows, half):
    slot, width = own.shape
    mv = inner.shape[0]
    block = width // (2 * n_dp)

    def group(s, tab):
        return lax.rem(tab[3 * n + 2] + s, n_dp)

    return pl.pallas_call(
        functools.partial(weights_kernel, n),
        out_shape=jax.ShapeDtypeStruct((2, rows, width // 4), BF16),
        grid_spec=pltpu.PrefetchScalarGridSpec(
            num_scalar_prefetch=1,
            grid=(n_dp,),
            in_specs=[
                pl.BlockSpec((slot, block), lambda s, tab: (0, 2 * group(s, tab) + half)),
                pl.BlockSpec((mv, block), lambda s, tab: (0, half * n_dp + group(s, tab))),
                pl.BlockSpec((mv, block), lambda s, tab: (0, group(s, tab))),
            ],
            out_specs=pl.BlockSpec((2, rows, block // 2), lambda s, tab: (0, 0, s)),
            scratch_shapes=[pltpu.VMEM((relayout_rows(slot, mv), block), F32)],
        ),
        compiler_params=params(),
        cost_estimate=cost(),
    )(tab, own, inner, outer)


def turned_kernel(piece, out):
    rows = piece.shape[1]
    for e in range(2):
        out[:, e * rows : (e + 1) * rows] = piece[e].astype(F32).T.astype(BF16)


def turned(piece):
    return pl.pallas_call(
        turned_kernel,
        out_shape=jax.ShapeDtypeStruct((piece.shape[2], 2 * piece.shape[1]), BF16),
        in_specs=[pl.BlockSpec(memory_space=pltpu.VMEM)],
        out_specs=pl.BlockSpec(memory_space=pltpu.VMEM),
        compiler_params=params(),
        cost_estimate=cost(),
    )(piece)


def forward_kernel(sent, tab, *refs):
    outs = refs[-4:-2] if sent else refs[-3:-2]
    pieces, (mine, other) = refs[: -4 - len(outs)], refs[-4 - len(outs) : -2 - len(outs)]
    hid, weights = refs[-2:]
    rows = mine.shape[1]
    tokens = pieces[0].shape[0]

    @pl.when(pl.program_id(0) == 0)
    def _():
        for i, piece in enumerate(pieces):
            hid[i * tokens : (i + 1) * tokens, :] = piece[...]

    weights[:rows, :] = mine[0]
    weights[rows:, :] = other[0]
    part = jnp.dot(hid[...], weights[...], preferred_element_type=F32).astype(BF16)
    for i in range(len(pieces)):
        block = part[i * tokens : (i + 1) * tokens, :]
        if not sent:
            outs[0][0, i] = block
        elif i < sent:
            outs[0][i, 0] = block
        else:
            outs[1][i - sent, 0] = block


def forward_chunk(tab, pieces, mine, other, sent, n_dp, at):
    tokens = pieces[0].shape[0]
    rows = mine.shape[1]
    block = mine.shape[2] // n_dp
    count = len(pieces)
    if sent:
        out_shape = [(sent, n_dp, tokens, block), (count - sent, n_dp, tokens, block)]
        out_specs = [pl.BlockSpec((shape[0], 1, tokens, block), lambda s: (0, s, 0, 0)) for shape in out_shape]
    else:
        out_shape = [(n_dp, count, tokens, block)]
        out_specs = [pl.BlockSpec((1, count, tokens, block), lambda s: (s, 0, 0, 0))]

    return pl.pallas_call(
        functools.partial(forward_kernel, sent),
        out_shape=[jax.ShapeDtypeStruct(shape, BF16) for shape in out_shape],
        grid=(n_dp,),
        in_specs=[SMEM]
        + [pl.BlockSpec(pieces[0].shape, lambda s: (0, 0))] * len(pieces)
        + [pl.BlockSpec((1, rows, block), lambda s: (at, 0, s))] * 2,
        out_specs=out_specs,
        scratch_shapes=[
            pltpu.VMEM((len(pieces) * tokens, 2 * rows), BF16),
            pltpu.VMEM((2 * rows, block), BF16),
        ],
        compiler_params=params(),
        cost_estimate=cost(),
    )(tab, *pieces, mine, other)


def fill_tokens(ht_refs, ht):
    tokens = ht_refs[0].shape[2]
    for i, ref in enumerate(ht_refs):
        ht[:, i * tokens : (i + 1) * tokens] = ref[0]


def fill_grads(parity, og_refs, places, og):
    for ref, (at, flip, count, *more) in zip(og_refs, places):
        rows = ref.shape[0]
        if flip is None:
            og[at : at + rows, :] = ref[...]
        else:
            shift = (parity if flip == 0 else 1 - parity) * count + more[0]
            og[pl.ds(pl.multiple_of(at + shift, rows), rows), :] = ref[...]


def partner_kernel(n, pieces, places, tab, *refs):
    ht_refs, og_refs, (out, ht, og) = refs[:pieces], refs[pieces:-3], refs[-3:]

    @pl.when(pl.program_id(0) == 0)
    def _():
        fill_tokens(ht_refs, ht)

    fill_grads(lax.rem(tab[3 * n + 2], 2), og_refs, places, og)
    out[...] = jnp.dot(ht[...], og[...], preferred_element_type=F32).astype(BF16)


def partner_grad(tab, pieces, grads, places, n):
    rows, tokens = pieces[0].shape[1:]
    width = grads[0].shape[1]
    block = min(width, 512)
    steps = width // block
    total = sum(g.shape[0] for g in grads)
    return pl.pallas_call(
        functools.partial(partner_kernel, n, len(pieces), places),
        out_shape=jax.ShapeDtypeStruct((rows, width), BF16),
        grid=(steps,),
        in_specs=[SMEM]
        + [pl.BlockSpec((1, rows, tokens), lambda i: (1, 0, 0))] * len(pieces)
        + [pl.BlockSpec((g.shape[0], block), lambda i: (0, i)) for g in grads],
        out_specs=pl.BlockSpec((rows, block), lambda i: (0, i)),
        scratch_shapes=[pltpu.VMEM((rows, total), BF16), pltpu.VMEM((total, block), BF16)],
        compiler_params=params(),
        cost_estimate=cost(),
    )(tab, *pieces, *grads)


def adam_kernel(n, pieces, places, scale, aliased, relayed, tab, *refs):
    ht_refs, refs = refs[:pieces], refs[pieces:]
    og_refs, refs = refs[: len(places)], refs[len(places) :]
    rest, own, (inner0, inner1, outer0, outer1, inner_both, outer_both) = refs[0], refs[1:4], refs[4:10]
    refs = refs[10:]
    relay, refs = refs[:relayed], refs[relayed + aliased :]
    outs, ht, og, gradient, moved = refs[0:3], refs[3], refs[4], refs[5], refs[6:9]
    slot, mv = own[0].shape[0], inner0.shape[0]
    block = og.shape[1]
    even = lax.rem(pl.program_id(0) // 2, 2) == 0

    @pl.when(pl.program_id(0) == 0)
    def _():
        fill_tokens(ht_refs, ht)

    fill_grads(lax.rem(tab[3 * n + 2], 2), og_refs, places, og)
    odd = lax.rem(tab[3 * n + 1], 2) == 1
    middle = (tab[3 * n + 1] == n // 2 - 1) | (tab[3 * n + 1] == n // 2)
    inner = chosen(even, from_ref(inner0), from_ref(inner1))
    outer = chosen(even, from_ref(outer0), from_ref(outer1))
    relayout(tab, n, from_ref(own[0]), chosen(odd, inner, outer), chosen(odd, outer, inner), slot, mv, moved[0])
    for i in range(2):
        columns = slice(i * block, (i + 1) * block)
        inner, outer = from_ref(inner_both, columns), from_ref(outer_both, columns)
        if relay:
            outer = chosen(middle, from_ref(relay[0], columns), outer)
            inner = chosen(True, inner, inner)
        relayout(tab, n, from_ref(own[i + 1]), chosen(odd, inner, outer), chosen(odd, outer, inner), slot, mv, moved[i + 1])
    start, end = new_range(tab, n, tab[3 * n + 1])
    gradient[...] = jnp.dot(ht[...], og[...], preferred_element_type=F32)
    gradient[...] = (gradient[...] + rest[...].astype(F32)) * scale
    size = piece_rows(slot, (24, 16, 8))
    for first in range(0, slot, size):
        grad = gradient[first : first + size, :]
        at = mv + slot + first
        master, first_old, second_old = (ref[at : at + size, :] for ref in moved)
        first_next = 0.9 * first_old + 0.1 * grad
        second_next = 0.95 * second_old + 0.05 * grad * grad
        master_next = master - 0.001 * (first_next / (jnp.sqrt(second_next) + 1e-08) + 0.1 * master)
        live = lax.broadcasted_iota(jnp.int32, grad.shape, 0) + first < end - start
        for out, value in zip(outs, (master_next, first_next, second_next)):
            out[first : first + size, :] = jnp.where(live, value, 0.0)


def adam_part(tab, pieces, grads, places, rest, own, edge, both, outs, n, n_dp, scale, part, parts):
    rows, tokens = pieces[0].shape[1:]
    slot, width = own[0].shape
    mv = both[0].shape[0]
    block = width // (4 * n_dp)
    steps = width // parts // block
    total = sum(g.shape[0] for g in grads)
    inner, outers = edge

    def column(i):
        return 0, part * steps + i

    def first(i):
        return 0, (part * steps + i) // 4 * 2 + i % 2

    def second(i):
        return 0, 2 * n_dp + (part * steps + i) // 4 * 2 + i % 2

    def inner_both(i):
        return 0, part * steps + i

    operands = [tab, *pieces, *grads, rest, *own, inner, inner, *outers, *both, *outs]
    return pl.pallas_call(
        functools.partial(adam_kernel, n, len(pieces), places, scale, len(outs), len(both) - 2),
        out_shape=[jax.ShapeDtypeStruct((slot, width), F32)] * 3,
        grid=(steps,),
        in_specs=[SMEM]
        + [pl.BlockSpec((1, rows, tokens), lambda i: (0, 0, 0))] * len(pieces)
        + [pl.BlockSpec((g.shape[0], block), column) for g in grads]
        + [pl.BlockSpec((rows, block), column)]
        + [pl.BlockSpec((slot, block), column)] * 3
        + [pl.BlockSpec((mv, block), first), pl.BlockSpec((mv, block), second)]
        + [pl.BlockSpec((mv, block), first)] * 2
        + [pl.BlockSpec((mv, 2 * block), inner_both)]
        + [pl.BlockSpec((mv, 2 * block), lambda i: (0, i))] * (len(both) - 1)
        + [pl.BlockSpec(memory_space=pl.ANY)] * len(outs),
        out_specs=[pl.BlockSpec((slot, block), column)] * 3,
        scratch_shapes=[
            pltpu.VMEM((rows, total), BF16),
            pltpu.VMEM((total, block), BF16),
            pltpu.VMEM((rows, block), F32),
        ]
        + [pltpu.VMEM((relayout_rows(slot, mv), block), F32)] * 3,
        input_output_aliases={len(operands) - 3 + i: i for i in range(3)} if outs else {},
        compiler_params=params(),
        cost_estimate=cost(),
    )(*operands)


def swap(value, mask):
    n = lax.axis_size("fsdp")
    return lax.ppermute(value, "fsdp", [(i, i ^ mask) for i in range(n)])


def swap_outer(value, middle=True):
    n = lax.axis_size("fsdp")
    pairs = [(i, i + 1 if i % 2 else i - 1) for i in range(1, n - 1)]
    return lax.ppermute(value, "fsdp", [(i, j) for i, j in pairs if middle or {i, j} != {3, 4}])


def relay_first(value):
    return lax.ppermute(value, "fsdp", [(3, 7), (4, 0)])


def relay_second(value):
    return lax.ppermute(value, "fsdp", [(7, 4), (0, 3)])


def turn(value, steps):
    n = lax.axis_size("dp")
    return lax.ppermute(value, "dp", [(i, (i + steps) % n) for i in range(n)])


def stage(*values):
    return lax.optimization_barrier(values)


def add(a, b):
    return (a.astype(F32) + b.astype(F32)).astype(BF16)


def local(gate, up, out_grad, master_old, moment1_old, moment2_old, old_bounds, new_bounds, rank_map):
    n, n_dp = lax.axis_size("fsdp"), lax.axis_size("dp")
    groups = n // 2
    square = groups == 4
    chunks, parts = 4, 4
    tokens, block_rows = gate.shape
    slot, width = master_old.shape[1:]
    rows = round_up(slot, 16)
    mv = round_up((block_rows // n + 1) // 2, 16)
    scale = 1.0 / math.sqrt(tokens * n)
    index = jnp.stack([lax.axis_index("fsdp"), lax.axis_index("dp")]).astype(jnp.int32)
    tab = jnp.concatenate([old_bounds[0], new_bounds[0], rank_map[0], index])
    own = [master_old[0], moment1_old[0], moment2_old[0]]
    half = tokens // 2
    parity = lax.rem(lax.axis_index("dp"), 2)
    mine_grad = lax.dynamic_slice_in_dim(out_grad, parity * half, half, 0)

    block = width // (2 * n_dp)
    small = block // 2
    steps = width // parts // small
    order = [2, 3, 0, 1] if square else list(range(1, groups)) + [0]
    sent = 2 if square else groups - 1

    def flip(value):
        return lax.ppermute(value, "dp", [(i, i ^ 1) for i in range(n_dp)])

    def forward(chunk):
        mine, other = weights[chunk // 2]
        by_dp = square and chunk == 1
        return forward_chunk(tab, [tokens_first[i] for i in order], mine, other, 0 if by_dp else sent, n_dp, chunk % 2)

    def first_sum(chunk):
        send = sends[chunk]
        if square:
            return [swap(send, 4)]
        return [swap(send[rel - 1], 2 * rel) for rel in range(1, groups)]

    def second_sum(chunk):
        return swap(add(keeps[chunk][1], came[chunk][0][1]), 2) if square else tab

    def summed(chunk, passed):
        total = keeps[chunk][0].astype(F32)
        if square:
            return total + came[chunk][0][0].astype(F32) + passed.astype(F32)
        for value in came[chunk]:
            total = total + value.astype(F32)
        return total

    def over_dp(total):
        low = total.astype(BF16)
        out = total[0]
        for turned_by in range(1, n_dp):
            out = out + turn(low[turned_by], turned_by).astype(F32)
        return out

    def step(part, outs):
        moved = (moving_inner, *moved_outer[part])
        return list(
            adam_part(tab, pieces, grads, places, partner, own, (inner, outers), moved, outs, n, n_dp, scale, part, parts)
        )

    inner, *outers = edges(
        tab, own[:1], n, mv, block, [[(2 * j + h) * block for j in range(n_dp)] for h in range(2)]
    )
    quarter = half // 2
    tab, inner, outers, mine_grad, quarters = stage(
        tab, inner, outers, mine_grad, [mine_grad[:quarter], mine_grad[quarter:]]
    )
    outers = list(outers)
    inner, outers[0] = swap(inner, 1), swap_outer(outers[0])
    windows = list(hidden_windows(tab, gate, up, n, rows))
    moving = list(
        edges(
            tab,
            own[1:],
            n,
            mv,
            small,
            [[(part * steps + i) * small for i in range(steps)] for part in range(parts)],
        )
    )
    grad_y = [swap(quarters[0], 4)] if square else []
    tab, inner, outers, mine_grad, grad_y, windows, moving = stage(
        tab, inner, outers, mine_grad, grad_y, windows, moving
    )

    outers, moving, grad_y = list(outers), list(moving), list(grad_y)
    outers[1] = swap_outer(outers[1])
    flips_y = []
    if square:
        grad_y.append(swap(quarters[1], 4))
        flips_y.append(flip(grad_y[0]))
    moving_inner = swap(moving[0], 1)
    mine = new_weights(tab, own[0], inner, outers[0], n, n_dp, rows, 0)
    tab, outers, mine_grad, grad_y, flips_y, windows, moving, moving_inner, mine = stage(
        tab, outers, mine_grad, grad_y, flips_y, windows, moving, moving_inner, mine
    )

    pieces, flips_y = list(windows), list(flips_y)
    for rel in range(1, groups):
        pieces[rel] = swap(pieces[rel], 2 * rel)
    weights = [(mine, swap(mine, 1))]
    if square:
        flips_y.append(flip(grad_y[1]))
    mine = new_weights(tab, own[0], inner, outers[1], n, n_dp, rows, 1)
    tokens_first = [turned(pieces[0])]
    tab, mine_grad, flips_y, moving, pieces, weights, mine, tokens_first = stage(
        tab, mine_grad, flips_y, moving, pieces, weights, mine, tokens_first
    )

    weights = list(weights) + [(mine, swap(mine, 1))]
    tokens_first = list(tokens_first) + [turned(piece) for piece in pieces[1:]]
    sends, keeps, came, totals = [None] * chunks, [None] * chunks, [None] * chunks, [None] * chunks
    sends[0], keeps[0] = forward(0)
    if square:
        (last,) = forward(1)
    else:
        sends[1], keeps[1] = forward(1)
        last = tab
    grad_x = swap(mine_grad, 2) if square else mine_grad
    relays = [relay_first(moving[2]), relay_first(moving[4])] if square else []
    tab, grad_x, moving, weights, sends, keeps, tokens_first, relays, last = stage(
        tab, grad_x, moving, weights, sends, keeps, tokens_first, relays, last
    )

    sends, keeps, relays = list(sends), list(keeps), list(relays)
    moved_outer = [(swap_outer(moving[1]),)]
    if square:
        relays[0] = relay_second(relays[0])
        grad_g, flip_x = swap(grad_x, 4), flip(grad_x)
    else:
        grad_g, flip_x = grad_x, grad_x
    turns = [turn(last[i], i) for i in range(2, n_dp, 2)] if square else []
    sends[2], keeps[2] = forward(2)
    sends[3], keeps[3] = forward(3)
    tab, grad_x, grad_g, flip_x, moving, moved_outer, sends, keeps, relays, turns, last = stage(
        tab, grad_x, grad_g, flip_x, moving, moved_outer, sends, keeps, relays, turns, last
    )

    sends, keeps, moved_outer, relays = list(sends), list(keeps), list(moved_outer), list(relays)
    moved_outer.append((swap_outer(moving[2], not square), *relays[:1]))
    came[0] = first_sum(0)
    if square:
        relays[1] = relay_second(relays[1])
    flip_g = flip(grad_g) if square else grad_g
    tab, flip_g, moving, moved_outer, sends, keeps, came, relays, last = stage(
        tab, flip_g, moving, moved_outer, sends, keeps, came, relays, last
    )

    keeps, came, moved_outer = list(keeps), list(came), list(moved_outer)
    if square:
        grads = [out_grad, grad_x, *grad_y, grad_g, flip_x, *flips_y, flip_g]
        places = [(0, None, tokens)]
        for which in range(2):
            places += [(tokens, which, half, 0), (2 * tokens, which, half, 0), (2 * tokens, which, half, quarter)]
            places += [(3 * tokens, which, half, 0)]
    else:
        grads = [out_grad] + [swap(out_grad, 2 * rel) for rel in range(1, groups)]
        places = [(i * tokens, None, tokens) for i in range(groups)]
    moved_outer.append((swap_outer(moving[3]),))
    came[2] = first_sum(2)
    totals[0] = second_sum(0)
    turns = list(turns)
    if square:
        turns += [turn(last[i], i) for i in range(1, n_dp, 2)]
    partner = partner_grad(tab, pieces, grads, places, n)
    tab, moving, moved_outer, sends, came, totals, partner, turns, last = stage(
        tab, moving, moved_outer, sends, came, totals, partner, turns, last
    )

    came, totals, moved_outer = list(came), list(totals), list(moved_outer)
    moved_outer.append((swap_outer(moving[4], not square), *relays[1:]))
    came[3] = first_sum(3)
    totals[2] = second_sum(2)
    partner, tab = stage(swap(partner, 1), tab)
    outs = step(1, step(0, []))
    tab, moved_outer, sends, came, totals, outs, turns = stage(
        tab, moved_outer, sends, came, totals, outs, turns
    )

    came, totals = list(came), list(totals)
    totals[3] = second_sum(3)
    if square:
        total = last[0].astype(F32)
        for value in turns:
            total = total + value.astype(F32)
        came[1] = [swap(total[:2].astype(BF16), 4)]
        keeps[1] = total[2:]
    else:
        came[1] = first_sum(1)
    both = over_dp(jnp.stack([summed(i, totals[i]) for i in (0, 2)], axis=1))
    outs = step(3, step(2, list(outs)))
    tab, came, totals, outs = stage(tab, came, totals, list(outs))

    totals = list(totals)
    total = summed(1, second_sum(1))
    results = [both[0], total if square else over_dp(total), both[1], over_dp(summed(3, totals[3]))]
    mlp_out = jnp.concatenate(results, axis=1)
    return mlp_out, outs[0][None], outs[1][None], outs[2][None]


def solution(mesh):
    placed = (
        P("fsdp", "dp"),
        P("fsdp", "dp"),
        P("fsdp", None),
        P("dp", "fsdp", None),
        P("dp", "fsdp", None),
        P("dp", "fsdp", None),
        P("dp", None),
        P("dp", None),
        P("dp", None),
    )
    return jax.shard_map(
        local,
        mesh=mesh,
        in_specs=placed,
        out_specs=(
            P("fsdp", "dp"),
            P("dp", "fsdp", None),
            P("dp", "fsdp", None),
            P("dp", "fsdp", None),
        ),
        check_vma=False,
    )
```

```python
import functools
import math

import jax
import jax.numpy as jnp
from jax import lax
from jax.experimental import pallas as pl
from jax.experimental.pallas import tpu as pltpu
from jax.sharding import PartitionSpec as P

BF16 = jnp.bfloat16
F32 = jnp.float32
VMEM_BYTES = 58 * 1024 * 1024
SMEM = pl.BlockSpec(memory_space=pltpu.SMEM)


def round_up(value, step):
    return -(-value // step) * step


def params():
    return pltpu.CompilerParams(vmem_limit_bytes=VMEM_BYTES)


def cost():
    return pl.CostEstimate(flops=1, bytes_accessed=1, transcendentals=0)


def old_range(tab, n, q):
    return tab[q], tab[q + 1]


def new_range(tab, n, q):
    k = tab[2 * n + 1 + q]
    return tab[n + 1 + jnp.minimum(k, n - 1)], tab[n + 1 + jnp.minimum(k + 1, n - 1)]


def shifted_rows(ref, start, rows):
    base = pl.multiple_of((start // 8) * 8, 8)
    rem = start - base
    x = ref[pl.ds(base, rows + 8), :]
    lanes = x.shape[1]
    y = pltpu.roll(x.reshape(rows // 8 + 1, 8, lanes), (8 - rem) % 8, 1)
    sublane = lax.broadcasted_iota(jnp.int32, (rows // 8, 8, lanes), 1)
    return jnp.where(sublane < 8 - rem, y[:-1], y[1:]).reshape(rows, lanes)


def piece_rows(rows, sizes=(48, 32, 24, 16, 8)):
    return next(size for size in sizes if rows % size == 0)


def rolled(x, rem):
    return pltpu.roll(x.reshape(x.shape[0] // 8, 8, x.shape[1]), rem, 1)


def place_rows(parts, dst, start, keep):
    base = pl.multiple_of((start // 8) * 8, 8)
    rem = start - base
    last = None
    at = 0
    for load, rows in parts:
        size = piece_rows(rows)
        for first in range(0, rows, size):
            y = rolled(load(first, size), rem)
            lanes = y.shape[2]
            if last is None:
                last = dst[pl.ds(base, 8), :].reshape(1, 8, lanes) if keep else y[:1]
            before = jnp.concatenate([last, y[:-1]]) if size > 8 else last
            sublane = lax.broadcasted_iota(jnp.int32, y.shape, 1)
            out = jnp.where(sublane < rem, before, y)
            dst[pl.ds(pl.multiple_of(base + at, 8), size), :] = out.reshape(size, lanes)
            last = y[-1:]
            at += size
    dst[pl.ds(pl.multiple_of(base + at, 8), 8), :] = last.reshape(8, last.shape[2])


def relayout(tab, n, own, left, right, slot, mv, dst):
    q = tab[3 * n + 1]
    old_start, old_end = old_range(tab, n, q)
    new_start, _ = new_range(tab, n, q)
    start = slot + jnp.clip(old_start - new_start, -slot, mv)
    place_rows([(left, mv), (own, slot)], dst, start, False)
    start = mv + slot + jnp.clip(old_end - new_start, -mv, slot)
    place_rows([(right, mv)], dst, start, True)


def from_ref(ref, columns=slice(None)):
    return lambda first, rows: ref[first : first + rows, columns]


def chosen(flag, a, b):
    return lambda first, rows: jnp.where(flag, a(first, rows), b(first, rows)).astype(F32)


def relayout_rows(slot, mv):
    return 2 * slot + 2 * mv + 32


def hidden_kernel(n, rows, tab, gate, up, *refs):
    outs, scratch = refs[:-1], refs[-1]
    tokens, width = gate.shape
    for first in range(0, width, 128):
        last = min(first + 128, width)
        g = gate[:, first:last].astype(F32)
        h = g / (1.0 + jnp.exp(-g)) * up[:, first:last].astype(F32)
        scratch[first:last, :] = h.T
    scratch[width:, :] = jnp.zeros((scratch.shape[0] - width, tokens), F32)
    q = tab[3 * n + 1]
    piece = piece_rows(rows, (48, 16))
    for rel, out in enumerate(outs):
        for other in range(2):
            start, _ = new_range(tab, n, q ^ (2 * rel + other))
            for row in range(0, rows, piece):
                out[other, row : row + piece, :] = shifted_rows(scratch, start + row, piece).astype(BF16)


def hidden_windows(tab, gate, up, n, rows):
    tokens, width = gate.shape
    shape = jax.ShapeDtypeStruct((2, rows, tokens), BF16)
    return pl.pallas_call(
        functools.partial(hidden_kernel, n, rows),
        out_shape=[shape] * (n // 2),
        in_specs=[SMEM, pl.BlockSpec(memory_space=pltpu.VMEM), pl.BlockSpec(memory_space=pltpu.VMEM)],
        out_specs=[pl.BlockSpec(memory_space=pltpu.VMEM)] * (n // 2),
        scratch_shapes=[pltpu.VMEM((round_up(width, 8) + rows + 8, tokens), F32)],
        compiler_params=params(),
        cost_estimate=cost(),
    )(tab, gate, up)


def edges_kernel(n, mv, count, block, starts, tab, *refs):
    ins, inner, outers, (head, tail, sems) = refs[:count], refs[count], refs[count + 1 : -3], refs[-3:]
    q = tab[3 * n + 1]
    odd = lax.rem(q, 2) == 1
    old_start, old_end = old_range(tab, n, q)
    live = old_end - old_start
    slot, width = ins[0].shape
    base = pl.multiple_of((jnp.clip(live - mv, 0, slot - mv - 8) // 8) * 8, 8)
    size = len(starts[0]) * count * block
    piece = piece_rows(mv, (48, 32, 16))
    work = []
    for part, blocks in enumerate(starts):
        for at, start in enumerate(blocks):
            for i in range(count):
                k = len(work)
                columns = pl.ds(start, block)
                first = pltpu.make_async_copy(ins[i].at[pl.ds(0, mv), columns], head.at[k], sems.at[k, 0])
                last = pltpu.make_async_copy(
                    ins[i].at[pl.ds(base, mv + 8), columns], tail.at[k, pl.ds(mv + 8, mv + 8)], sems.at[k, 1]
                )
                work.append((first, last, part, (at * count + i) * block))
    for first, last, _, _ in work:
        first.start()
        last.start()
    for k, (first, last, part, place) in enumerate(work):
        first.wait()
        last.wait()
        inner_place = place + part * size
        for row in range(0, mv, piece):
            rows = slice(row, row + piece)
            top = head[k, rows, :]
            end = shifted_rows(tail.at[k], live + 8 - base + row, piece)
            outers[part][rows, place : place + block] = jnp.where(odd, end, top).astype(BF16)
            inner[rows, inner_place : inner_place + block] = jnp.where(odd, top, end).astype(BF16)


def edges(tab, arrays, n, mv, block, starts):
    count = len(arrays)
    pieces = len(starts) * len(starts[0]) * count
    width = pieces * block
    return pl.pallas_call(
        functools.partial(edges_kernel, n, mv, count, block, starts),
        out_shape=[jax.ShapeDtypeStruct((mv, width), BF16)]
        + [jax.ShapeDtypeStruct((mv, width // len(starts)), BF16)] * len(starts),
        in_specs=[SMEM] + [pl.BlockSpec(memory_space=pl.ANY)] * count,
        out_specs=[pl.BlockSpec(memory_space=pltpu.VMEM)] * (1 + len(starts)),
        scratch_shapes=[
            pltpu.VMEM((pieces, mv, block), F32),
            pltpu.VMEM((pieces, 2 * mv + 32, block), F32),
            pltpu.SemaphoreType.DMA((pieces, 2)),
        ],
        compiler_params=params(),
        cost_estimate=cost(),
    )(tab, *arrays)


def weights_kernel(n, tab, own, inner, outer, out, dst):
    slot, mv = own.shape[0], inner.shape[0]
    q = tab[3 * n + 1]
    odd = lax.rem(q, 2) == 1
    left = chosen(odd, from_ref(inner), from_ref(outer))
    right = chosen(odd, from_ref(outer), from_ref(inner))
    relayout(tab, n, from_ref(own), left, right, slot, mv, dst)
    start, end = new_range(tab, n, q)
    block = out.shape[2]
    size = piece_rows(out.shape[1], (48, 32, 16))
    for first in range(0, out.shape[1], size):
        kept = dst[mv + slot + first : mv + slot + first + size, :]
        row = lax.broadcasted_iota(jnp.int32, kept.shape, 0) + first
        kept = jnp.where(row < end - start, kept, 0.0).astype(BF16)
        for i in range(out.shape[0]):
            out[i, first : first + size, :] = kept[:, i * block : (i + 1) * block]


def new_weights(tab, own, inner, outer, n, n_dp, rows, half):
    slot, width = own.shape
    mv = inner.shape[0]
    block = width // (2 * n_dp)

    def group(s, tab):
        return lax.rem(tab[3 * n + 2] + s, n_dp)

    return pl.pallas_call(
        functools.partial(weights_kernel, n),
        out_shape=jax.ShapeDtypeStruct((2, rows, width // 4), BF16),
        grid_spec=pltpu.PrefetchScalarGridSpec(
            num_scalar_prefetch=1,
            grid=(n_dp,),
            in_specs=[
                pl.BlockSpec((slot, block), lambda s, tab: (0, 2 * group(s, tab) + half)),
                pl.BlockSpec((mv, block), lambda s, tab: (0, group(s, tab))),
                pl.BlockSpec((mv, block), lambda s, tab: (0, group(s, tab))),
            ],
            out_specs=pl.BlockSpec((2, rows, block // 2), lambda s, tab: (0, 0, s)),
            scratch_shapes=[pltpu.VMEM((relayout_rows(slot, mv), block), F32)],
        ),
        compiler_params=params(),
        cost_estimate=cost(),
    )(tab, own, inner, outer)


def turned_kernel(piece, out):
    rows = piece.shape[1]
    for e in range(2):
        out[:, e * rows : (e + 1) * rows] = piece[e].astype(F32).T.astype(BF16)


def turned(piece):
    return pl.pallas_call(
        turned_kernel,
        out_shape=jax.ShapeDtypeStruct((piece.shape[2], 2 * piece.shape[1]), BF16),
        in_specs=[pl.BlockSpec(memory_space=pltpu.VMEM)],
        out_specs=pl.BlockSpec(memory_space=pltpu.VMEM),
        compiler_params=params(),
        cost_estimate=cost(),
    )(piece)


def forward_kernel(sent, tab, *refs):
    outs = refs[-4:-2] if sent else refs[-3:-2]
    pieces, (mine, other) = refs[: -4 - len(outs)], refs[-4 - len(outs) : -2 - len(outs)]
    hid, weights = refs[-2:]
    rows = mine.shape[1]
    tokens = pieces[0].shape[0]

    @pl.when(pl.program_id(0) == 0)
    def _():
        for i, piece in enumerate(pieces):
            hid[i * tokens : (i + 1) * tokens, :] = piece[...]

    weights[:rows, :] = mine[0]
    weights[rows:, :] = other[0]
    part = jnp.dot(hid[...], weights[...], preferred_element_type=F32).astype(BF16)
    for i in range(len(pieces)):
        block = part[i * tokens : (i + 1) * tokens, :]
        if not sent:
            outs[0][0, i] = block
        elif i < sent:
            outs[0][i, 0] = block
        else:
            outs[1][i - sent, 0] = block


def forward_chunk(tab, pieces, mine, other, sent, n_dp, at):
    tokens = pieces[0].shape[0]
    rows = mine.shape[1]
    block = mine.shape[2] // n_dp
    count = len(pieces)
    if sent:
        out_shape = [(sent, n_dp, tokens, block), (count - sent, n_dp, tokens, block)]
        out_specs = [pl.BlockSpec((shape[0], 1, tokens, block), lambda s: (0, s, 0, 0)) for shape in out_shape]
    else:
        out_shape = [(n_dp, count, tokens, block)]
        out_specs = [pl.BlockSpec((1, count, tokens, block), lambda s: (s, 0, 0, 0))]

    return pl.pallas_call(
        functools.partial(forward_kernel, sent),
        out_shape=[jax.ShapeDtypeStruct(shape, BF16) for shape in out_shape],
        grid=(n_dp,),
        in_specs=[SMEM]
        + [pl.BlockSpec(pieces[0].shape, lambda s: (0, 0))] * len(pieces)
        + [pl.BlockSpec((1, rows, block), lambda s: (at, 0, s))] * 2,
        out_specs=out_specs,
        scratch_shapes=[
            pltpu.VMEM((len(pieces) * tokens, 2 * rows), BF16),
            pltpu.VMEM((2 * rows, block), BF16),
        ],
        compiler_params=params(),
        cost_estimate=cost(),
    )(tab, *pieces, mine, other)


def fill_tokens(ht_refs, ht):
    tokens = ht_refs[0].shape[2]
    for i, ref in enumerate(ht_refs):
        ht[:, i * tokens : (i + 1) * tokens] = ref[0]


def fill_grads(parity, og_refs, places, og):
    refs = iter(og_refs)
    for at, flip, half, more, filled, rows in places:
        value = next(refs)[...] if filled else jnp.zeros((rows, og.shape[1]), og.dtype)
        if flip is None:
            og[at : at + rows, :] = value
        else:
            shift = (parity if flip == 0 else 1 - parity) * half + more
            og[pl.ds(pl.multiple_of(at + shift, rows), rows), :] = value


def partner_kernel(n, pieces, places, tab, *refs):
    ht_refs, og_refs, (out, ht, og) = refs[:pieces], refs[pieces:-3], refs[-3:]

    @pl.when(pl.program_id(0) == 0)
    def _():
        fill_tokens(ht_refs, ht)

    fill_grads(lax.rem(tab[3 * n + 2], 2), og_refs, places, og)
    out[...] = jnp.dot(ht[...], og[...], preferred_element_type=F32).astype(BF16)


def partner_grad(tab, pieces, grads, places, n):
    rows, tokens = pieces[0].shape[1:]
    width = grads[0].shape[1]
    block = min(width, 512)
    steps = width // block
    total = sum(place[5] for place in places)
    return pl.pallas_call(
        functools.partial(partner_kernel, n, len(pieces), places),
        out_shape=jax.ShapeDtypeStruct((rows, width), BF16),
        grid=(steps,),
        in_specs=[SMEM]
        + [pl.BlockSpec((1, rows, tokens), lambda i: (1, 0, 0))] * len(pieces)
        + [pl.BlockSpec((g.shape[0], block), lambda i: (0, i)) for g in grads],
        out_specs=pl.BlockSpec((rows, block), lambda i: (0, i)),
        scratch_shapes=[pltpu.VMEM((rows, total), BF16), pltpu.VMEM((total, block), BF16)],
        compiler_params=params(),
        cost_estimate=cost(),
    )(tab, *pieces, *grads)


def adam_kernel(n, pieces, grads, places, scale, aliased, relayed, tab, *refs):
    ht_refs, refs = refs[:pieces], refs[pieces:]
    og_refs, refs = refs[:grads], refs[grads:]
    rest, own, (inner0, inner1, outer0, outer1, inner_both, outer_both) = refs[0], refs[1:4], refs[4:10]
    refs = refs[10:]
    relay, refs = refs[:relayed], refs[relayed + aliased :]
    outs, ht, og, gradient, moved = refs[0:3], refs[3], refs[4], refs[5], refs[6:9]
    slot, mv = own[0].shape[0], inner0.shape[0]
    block = og.shape[1]
    even = lax.rem(pl.program_id(0) // 2, 2) == 0

    @pl.when(pl.program_id(0) == 0)
    def _():
        fill_tokens(ht_refs, ht)

    fill_grads(lax.rem(tab[3 * n + 2], 2), og_refs, places, og)
    odd = lax.rem(tab[3 * n + 1], 2) == 1
    middle = (tab[3 * n + 1] == n // 2 - 1) | (tab[3 * n + 1] == n // 2)
    inner = chosen(even, from_ref(inner0), from_ref(inner1))
    outer = chosen(even, from_ref(outer0), from_ref(outer1))
    relayout(tab, n, from_ref(own[0]), chosen(odd, inner, outer), chosen(odd, outer, inner), slot, mv, moved[0])
    for i in range(2):
        columns = slice(i * block, (i + 1) * block)
        inner, outer = from_ref(inner_both, columns), from_ref(outer_both, columns)
        if relay:
            outer = chosen(middle, from_ref(relay[0], columns), outer)
            inner = chosen(True, inner, inner)
        relayout(tab, n, from_ref(own[i + 1]), chosen(odd, inner, outer), chosen(odd, outer, inner), slot, mv, moved[i + 1])
    start, end = new_range(tab, n, tab[3 * n + 1])
    gradient[...] = jnp.dot(ht[...], og[...], preferred_element_type=F32)
    gradient[...] = (gradient[...] + rest[...].astype(F32)) * scale
    size = piece_rows(slot, (24, 16, 8))
    for first in range(0, slot, size):
        grad = gradient[first : first + size, :]
        at = mv + slot + first
        master, first_old, second_old = (ref[at : at + size, :] for ref in moved)
        first_next = 0.9 * first_old + 0.1 * grad
        second_next = 0.95 * second_old + 0.05 * grad * grad
        master_next = master - 0.001 * (first_next / (jnp.sqrt(second_next) + 1e-08) + 0.1 * master)
        live = lax.broadcasted_iota(jnp.int32, grad.shape, 0) + first < end - start
        for out, value in zip(outs, (master_next, first_next, second_next)):
            out[first : first + size, :] = jnp.where(live, value, 0.0)


def adam_part(tab, pieces, grads, places, rest, own, edge, both, outs, n, n_dp, scale, part, parts):
    rows, tokens = pieces[0].shape[1:]
    slot, width = own[0].shape
    mv = both[0].shape[0]
    block = width // (4 * n_dp)
    steps = width // parts // block
    total = sum(place[5] for place in places)
    inners, outers = edge

    def column(i):
        return 0, part * steps + i

    def first(i):
        return 0, (part * steps + i) // 4 * 2 + i % 2

    def inner_both(i):
        return 0, part * steps + i

    operands = [tab, *pieces, *grads, rest, *own, *inners, *outers, *both, *outs]
    return pl.pallas_call(
        functools.partial(adam_kernel, n, len(pieces), len(grads), places, scale, len(outs), len(both) - 2),
        out_shape=[jax.ShapeDtypeStruct((slot, width), F32)] * 3,
        grid=(steps,),
        in_specs=[SMEM]
        + [pl.BlockSpec((1, rows, tokens), lambda i: (0, 0, 0))] * len(pieces)
        + [pl.BlockSpec((g.shape[0], block), column) for g in grads]
        + [pl.BlockSpec((rows, block), column)]
        + [pl.BlockSpec((slot, block), column)] * 3
        + [pl.BlockSpec((mv, block), first)] * 4
        + [pl.BlockSpec((mv, 2 * block), inner_both)]
        + [pl.BlockSpec((mv, 2 * block), lambda i: (0, i))] * (len(both) - 1)
        + [pl.BlockSpec(memory_space=pl.ANY)] * len(outs),
        out_specs=[pl.BlockSpec((slot, block), column)] * 3,
        scratch_shapes=[
            pltpu.VMEM((rows, total), BF16),
            pltpu.VMEM((total, block), BF16),
            pltpu.VMEM((rows, block), F32),
        ]
        + [pltpu.VMEM((relayout_rows(slot, mv), block), F32)] * 3,
        input_output_aliases={len(operands) - 3 + i: i for i in range(3)} if outs else {},
        compiler_params=params(),
        cost_estimate=cost(),
    )(*operands)


def swap(value, mask):
    n = lax.axis_size("fsdp")
    return lax.ppermute(value, "fsdp", [(i, i ^ mask) for i in range(n)])


def swap_outer(value, middle=True):
    n = lax.axis_size("fsdp")
    pairs = [(i, i + 1 if i % 2 else i - 1) for i in range(1, n - 1)]
    return lax.ppermute(value, "fsdp", [(i, j) for i, j in pairs if middle or {i, j} != {3, 4}])


def relay_first(value):
    return lax.ppermute(value, "fsdp", [(3, 7), (4, 0)])


def relay_second(value):
    return lax.ppermute(value, "fsdp", [(7, 4), (0, 3)])


def turn(value, steps):
    n = lax.axis_size("dp")
    return lax.ppermute(value, "dp", [(i, (i + steps) % n) for i in range(n)])


def stage(*values):
    return lax.optimization_barrier(values)


def add(a, b):
    return (a.astype(F32) + b.astype(F32)).astype(BF16)


def local(gate, up, out_grad, master_old, moment1_old, moment2_old, old_bounds, new_bounds, rank_map):
    n, n_dp = lax.axis_size("fsdp"), lax.axis_size("dp")
    groups = n // 2
    square = groups == 4
    chunks, parts = 4, 4
    tokens, block_rows = gate.shape
    slot, width = master_old.shape[1:]
    rows = round_up(slot, 16)
    mv = round_up((block_rows // n + 1) // 2, 16)
    scale = 1.0 / math.sqrt(tokens * n)
    index = jnp.stack([lax.axis_index("fsdp"), lax.axis_index("dp")]).astype(jnp.int32)
    tab = jnp.concatenate([old_bounds[0], new_bounds[0], rank_map[0], index])
    own = [master_old[0], moment1_old[0], moment2_old[0]]
    half = tokens // 2
    parity = lax.rem(lax.axis_index("dp"), 2)

    block = width // (2 * n_dp)
    small = block // 2
    steps = width // parts // small
    order = [2, 3, 0, 1] if square else list(range(1, groups)) + [0]
    sent = 2 if square else groups - 1

    def flip(value):
        return lax.ppermute(value, "dp", [(i, i ^ 1) for i in range(n_dp)])

    def forward(chunk):
        mine, other = weights[chunk // 2]
        by_dp = square and chunk == 1
        return forward_chunk(tab, [tokens_first[i] for i in order], mine, other, 0 if by_dp else sent, n_dp, chunk % 2)

    def first_sum(chunk):
        send = sends[chunk]
        if square:
            return [swap(send, 4)]
        return [swap(send[rel - 1], 2 * rel) for rel in range(1, groups)]

    def second_sum(chunk):
        return swap(add(keeps[chunk][1], came[chunk][0][1]), 2) if square else tab

    def summed(chunk, passed):
        total = keeps[chunk][0].astype(F32)
        if square:
            return total + came[chunk][0][0].astype(F32) + passed.astype(F32)
        for value in came[chunk]:
            total = total + value.astype(F32)
        return total

    def over_dp(total):
        low = total.astype(BF16)
        out = total[0]
        for turned_by in range(1, n_dp):
            out = out + turn(low[turned_by], turned_by).astype(F32)
        return out

    def step(part, outs):
        moved = (moving_inner, *moved_outer[part])
        return list(
            adam_part(tab, tokens_of, grads, places, partner, own, (inners, outers), moved, outs, n, n_dp, scale, part, parts)
        )

    def master_edges(tab, h):
        inner, outer = edges(tab, own[:1], n, mv, block, [[(2 * j + h) * block for j in range(n_dp)]])
        return inner, outer

    quarter = half // 2
    inner, outer = master_edges(tab, 0)
    tab, inner, outer, out_grad = stage(tab, inner, outer, out_grad)
    mine_grad = lax.dynamic_slice_in_dim(out_grad, parity * half, half, 0)
    quarters = [lax.dynamic_slice_in_dim(out_grad, parity * half + at, quarter, 0) for at in (0, quarter)]
    inners, outers = [swap(inner, 1)], [swap_outer(outer)]
    inner, outer = master_edges(tab, 1)
    inners.append(inner)
    outers.append(outer)
    windows = list(hidden_windows(tab, gate, up, n, rows))
    moving = list(
        edges(
            tab,
            own[1:],
            n,
            mv,
            small,
            [[(part * steps + i) * small for i in range(steps)] for part in range(parts)],
        )
    )
    grad_y = [swap(quarters[0], 4)] if square else []
    tab, inners, outers, mine_grad, quarters, grad_y, windows, moving = stage(
        tab, inners, outers, mine_grad, quarters, grad_y, windows, moving
    )

    inners, outers, moving, grad_y = list(inners), list(outers), list(moving), list(grad_y)
    outers[1] = swap_outer(outers[1])
    inners[1] = swap(inners[1], 1)
    flips_y = []
    if square:
        grad_y.append(swap(quarters[1], 4))
        flips_y.append(flip(grad_y[0]))
    moving_inner = swap(moving[0], 1)
    mine = new_weights(tab, own[0], inners[0], outers[0], n, n_dp, rows, 0)
    tab, inners, outers, mine_grad, grad_y, flips_y, windows, moving, moving_inner, mine = stage(
        tab, inners, outers, mine_grad, grad_y, flips_y, windows, moving, moving_inner, mine
    )

    pieces, flips_y = list(windows), list(flips_y)
    for rel in range(1, groups):
        pieces[rel] = swap(pieces[rel], 2 * rel)
    weights = [(mine, swap(mine, 1))]
    if square:
        flips_y.append(flip(grad_y[1]))
    mine = new_weights(tab, own[0], inners[1], outers[1], n, n_dp, rows, 1)
    tokens_first = [turned(pieces[0])]
    tab, mine_grad, flips_y, moving, pieces, weights, mine, tokens_first = stage(
        tab, mine_grad, flips_y, moving, pieces, weights, mine, tokens_first
    )

    weights = list(weights) + [(mine, swap(mine, 1))]
    tokens_first = list(tokens_first) + [turned(piece) for piece in pieces[1:]]
    sends, keeps, came, totals = [None] * chunks, [None] * chunks, [None] * chunks, [None] * chunks
    sends[0], keeps[0] = forward(0)
    if square:
        (last,) = forward(1)
    else:
        sends[1], keeps[1] = forward(1)
        last = tab
    grad_x = swap(mine_grad, 2) if square else mine_grad
    relays = [relay_first(moving[2]), relay_first(moving[4])] if square else []
    tab, grad_x, moving, weights, sends, keeps, tokens_first, relays, last = stage(
        tab, grad_x, moving, weights, sends, keeps, tokens_first, relays, last
    )

    sends, keeps, relays = list(sends), list(keeps), list(relays)
    moved_outer = [(swap_outer(moving[1]),)]
    if square:
        relays[0] = relay_second(relays[0])
        grad_g, flip_x = swap(grad_x, 4), flip(grad_x)
    else:
        grad_g, flip_x = grad_x, grad_x
    turns = [turn(last[i], i) for i in range(2, n_dp, 2)] if square else []
    sends[2], keeps[2] = forward(2)
    sends[3], keeps[3] = forward(3)
    tab, grad_x, grad_g, flip_x, moving, moved_outer, sends, keeps, relays, turns, last = stage(
        tab, grad_x, grad_g, flip_x, moving, moved_outer, sends, keeps, relays, turns, last
    )

    sends, keeps, moved_outer, relays = list(sends), list(keeps), list(moved_outer), list(relays)
    moved_outer.append((swap_outer(moving[2], not square), *relays[:1]))
    came[0] = first_sum(0)
    if square:
        relays[1] = relay_second(relays[1])
    flip_g = flip(grad_g) if square else grad_g
    tokens_of = pieces
    if square:
        grads = [out_grad, grad_x, *grad_y, grad_g, flip_x, *flips_y]
        places = [(0, None, tokens, 0, True, tokens)]
        for which in range(2):
            places += [(tokens, which, half, 0, True, half)]
            places += [(2 * tokens, which, half, more, True, quarter) for more in (0, quarter)]
            places += [(3 * tokens, which, half, 0, which == 0, half)]
        tokens_of = pieces + [swap(pieces[3][1], 1)[None]]
    else:
        grads = [out_grad] + [swap(out_grad, 2 * rel) for rel in range(1, groups)]
        places = [(i * tokens, None, tokens, 0, True, tokens) for i in range(groups)]
    partner = partner_grad(tab, pieces, grads, places, n)
    tab, flip_g, moving, moved_outer, sends, keeps, came, relays, tokens_of, partner = stage(
        tab, flip_g, moving, moved_outer, sends, keeps, came, relays, tokens_of, partner
    )

    keeps, came, moved_outer = list(keeps), list(came), list(moved_outer)
    moved_outer.append((swap_outer(moving[3]),))
    came[2] = first_sum(2)
    totals[0] = second_sum(0)
    partner = swap(partner, 1)
    if square:
        partner, flip_core, tab = stage(partner, swap(flip_g, 1), tab)
        grads = grads + [flip_g, flip_core]
        places = places[:-1] + [(3 * tokens, 1, half, 0, True, half)]
        places += [(4 * tokens, 0, half, 0, False, half), (4 * tokens, 1, half, 0, True, half)]
    else:
        partner, tab = stage(partner, tab)
    outs = step(1, step(0, []))
    tab, moving, moved_outer, sends, came, totals, outs, last = stage(
        tab, moving, moved_outer, sends, came, totals, outs, last
    )

    came, totals, moved_outer = list(came), list(totals), list(moved_outer)
    moved_outer.append((swap_outer(moving[4], not square), *relays[1:]))
    came[3] = first_sum(3)
    totals[2] = second_sum(2)
    turns = list(turns)
    if square:
        turns += [turn(last[i], i) for i in range(1, n_dp, 2)]
    outs = step(2, list(outs))
    tab, moved_outer, sends, came, totals, outs, turns = stage(
        tab, moved_outer, sends, came, totals, outs, turns
    )

    came, totals = list(came), list(totals)
    totals[3] = second_sum(3)
    if square:
        total = last[0].astype(F32)
        for value in turns:
            total = total + value.astype(F32)
        came[1] = [swap(total[:2].astype(BF16), 4)]
        keeps[1] = total[2:]
    else:
        came[1] = first_sum(1)
    both = over_dp(jnp.stack([summed(i, totals[i]) for i in (0, 2)], axis=1))
    outs = step(3, list(outs))
    tab, came, totals, outs = stage(tab, came, totals, list(outs))

    totals = list(totals)
    total = summed(1, second_sum(1))
    results = [both[0], total if square else over_dp(total), both[1], over_dp(summed(3, totals[3]))]
    mlp_out = jnp.concatenate(results, axis=1)
    return mlp_out, outs[0][None], outs[1][None], outs[2][None]


def solution(mesh):
    placed = (
        P("fsdp", "dp"),
        P("fsdp", "dp"),
        P("fsdp", None),
        P("dp", "fsdp", None),
        P("dp", "fsdp", None),
        P("dp", "fsdp", None),
        P("dp", None),
        P("dp", None),
        P("dp", None),
    )
    return jax.shard_map(
        local,
        mesh=mesh,
        in_specs=placed,
        out_specs=(
            P("fsdp", "dp"),
            P("dp", "fsdp", None),
            P("dp", "fsdp", None),
            P("dp", "fsdp", None),
        ),
        check_vma=False,
    )
```

```python
import functools
import math

import jax
import jax.numpy as jnp
from jax import lax
from jax.experimental import pallas as pl
from jax.experimental.pallas import tpu as pltpu
from jax.sharding import PartitionSpec as P

BF16 = jnp.bfloat16
F32 = jnp.float32
VMEM_BYTES = 58 * 1024 * 1024
SMEM = pl.BlockSpec(memory_space=pltpu.SMEM)


def round_up(value, step):
    return -(-value // step) * step


def params():
    return pltpu.CompilerParams(vmem_limit_bytes=VMEM_BYTES)


def cost():
    return pl.CostEstimate(flops=1, bytes_accessed=1, transcendentals=0)


def old_range(tab, n, q):
    return tab[q], tab[q + 1]


def new_range(tab, n, q):
    k = tab[2 * n + 1 + q]
    return tab[n + 1 + jnp.minimum(k, n - 1)], tab[n + 1 + jnp.minimum(k + 1, n - 1)]


def shifted_rows(ref, start, rows):
    base = pl.multiple_of((start // 8) * 8, 8)
    rem = start - base
    x = ref[pl.ds(base, rows + 8), :]
    lanes = x.shape[1]
    y = pltpu.roll(x.reshape(rows // 8 + 1, 8, lanes), (8 - rem) % 8, 1)
    sublane = lax.broadcasted_iota(jnp.int32, (rows // 8, 8, lanes), 1)
    return jnp.where(sublane < 8 - rem, y[:-1], y[1:]).reshape(rows, lanes)


def piece_rows(rows, sizes=(48, 32, 24, 16, 8)):
    return next(size for size in sizes if rows % size == 0)


def rolled(x, rem):
    return pltpu.roll(x.reshape(x.shape[0] // 8, 8, x.shape[1]), rem, 1)


def place_rows(parts, dst, start, keep):
    base = pl.multiple_of((start // 8) * 8, 8)
    rem = start - base
    last = None
    at = 0
    for load, rows in parts:
        size = piece_rows(rows)
        for first in range(0, rows, size):
            y = rolled(load(first, size), rem)
            lanes = y.shape[2]
            if last is None:
                last = dst[pl.ds(base, 8), :].reshape(1, 8, lanes) if keep else y[:1]
            before = jnp.concatenate([last, y[:-1]]) if size > 8 else last
            sublane = lax.broadcasted_iota(jnp.int32, y.shape, 1)
            out = jnp.where(sublane < rem, before, y)
            dst[pl.ds(pl.multiple_of(base + at, 8), size), :] = out.reshape(size, lanes)
            last = y[-1:]
            at += size
    dst[pl.ds(pl.multiple_of(base + at, 8), 8), :] = last.reshape(8, last.shape[2])


def relayout(tab, n, own, left, right, slot, mv, dst):
    q = tab[3 * n + 1]
    old_start, old_end = old_range(tab, n, q)
    new_start, _ = new_range(tab, n, q)
    start = slot + jnp.clip(old_start - new_start, -slot, mv)
    place_rows([(left, mv), (own, slot)], dst, start, False)
    start = mv + slot + jnp.clip(old_end - new_start, -mv, slot)
    place_rows([(right, mv)], dst, start, True)


def from_ref(ref, columns=slice(None)):
    return lambda first, rows: ref[first : first + rows, columns]


def chosen(flag, a, b):
    return lambda first, rows: jnp.where(flag, a(first, rows), b(first, rows)).astype(F32)


def relayout_rows(slot, mv):
    return 2 * slot + 2 * mv + 32


def hidden_kernel(n, rows, tab, gate, up, *refs):
    outs, scratch = refs[:-1], refs[-1]
    tokens, width = gate.shape
    for first in range(0, width, 128):
        last = min(first + 128, width)
        g = gate[:, first:last].astype(F32)
        h = g / (1.0 + jnp.exp(-g)) * up[:, first:last].astype(F32)
        scratch[first:last, :] = h.T
    scratch[width:, :] = jnp.zeros((scratch.shape[0] - width, tokens), F32)
    q = tab[3 * n + 1]
    piece = piece_rows(rows, (48, 16))
    for rel, out in enumerate(outs):
        for other in range(2):
            start, _ = new_range(tab, n, q ^ (2 * rel + other))
            for row in range(0, rows, piece):
                out[other, row : row + piece, :] = shifted_rows(scratch, start + row, piece).astype(BF16)


def hidden_windows(tab, gate, up, n, rows):
    tokens, width = gate.shape
    shape = jax.ShapeDtypeStruct((2, rows, tokens), BF16)
    return pl.pallas_call(
        functools.partial(hidden_kernel, n, rows),
        out_shape=[shape] * (n // 2),
        in_specs=[SMEM, pl.BlockSpec(memory_space=pltpu.VMEM), pl.BlockSpec(memory_space=pltpu.VMEM)],
        out_specs=[pl.BlockSpec(memory_space=pltpu.VMEM)] * (n // 2),
        scratch_shapes=[pltpu.VMEM((round_up(width, 8) + rows + 8, tokens), F32)],
        compiler_params=params(),
        cost_estimate=cost(),
    )(tab, gate, up)


def edges_kernel(n, mv, count, block, starts, tab, *refs):
    ins, inner, outers, (head, tail, sems) = refs[:count], refs[count], refs[count + 1 : -3], refs[-3:]
    q = tab[3 * n + 1]
    odd = lax.rem(q, 2) == 1
    old_start, old_end = old_range(tab, n, q)
    live = old_end - old_start
    slot, width = ins[0].shape
    base = pl.multiple_of((jnp.clip(live - mv, 0, slot - mv - 8) // 8) * 8, 8)
    size = len(starts[0]) * count * block
    piece = piece_rows(mv, (48, 32, 16))
    work = []
    for part, blocks in enumerate(starts):
        for at, start in enumerate(blocks):
            for i in range(count):
                k = len(work)
                columns = pl.ds(start, block)
                first = pltpu.make_async_copy(ins[i].at[pl.ds(0, mv), columns], head.at[k], sems.at[k, 0])
                last = pltpu.make_async_copy(
                    ins[i].at[pl.ds(base, mv + 8), columns], tail.at[k, pl.ds(mv + 8, mv + 8)], sems.at[k, 1]
                )
                work.append((first, last, part, (at * count + i) * block))
    for first, last, _, _ in work:
        first.start()
        last.start()
    for k, (first, last, part, place) in enumerate(work):
        first.wait()
        last.wait()
        inner_place = place + part * size
        for row in range(0, mv, piece):
            rows = slice(row, row + piece)
            top = head[k, rows, :]
            end = shifted_rows(tail.at[k], live + 8 - base + row, piece)
            outers[part][rows, place : place + block] = jnp.where(odd, end, top).astype(BF16)
            inner[rows, inner_place : inner_place + block] = jnp.where(odd, top, end).astype(BF16)


def edges(tab, arrays, n, mv, block, starts):
    count = len(arrays)
    pieces = len(starts) * len(starts[0]) * count
    width = pieces * block
    return pl.pallas_call(
        functools.partial(edges_kernel, n, mv, count, block, starts),
        out_shape=[jax.ShapeDtypeStruct((mv, width), BF16)]
        + [jax.ShapeDtypeStruct((mv, width // len(starts)), BF16)] * len(starts),
        in_specs=[SMEM] + [pl.BlockSpec(memory_space=pl.ANY)] * count,
        out_specs=[pl.BlockSpec(memory_space=pltpu.VMEM)] * (1 + len(starts)),
        scratch_shapes=[
            pltpu.VMEM((pieces, mv, block), F32),
            pltpu.VMEM((pieces, 2 * mv + 32, block), F32),
            pltpu.SemaphoreType.DMA((pieces, 2)),
        ],
        compiler_params=params(),
        cost_estimate=cost(),
    )(tab, *arrays)


def weights_kernel(n, tab, own, inner, outer, out, dst):
    slot, mv = own.shape[0], inner.shape[0]
    q = tab[3 * n + 1]
    odd = lax.rem(q, 2) == 1
    left = chosen(odd, from_ref(inner), from_ref(outer))
    right = chosen(odd, from_ref(outer), from_ref(inner))
    relayout(tab, n, from_ref(own), left, right, slot, mv, dst)
    start, end = new_range(tab, n, q)
    block = out.shape[2]
    size = piece_rows(out.shape[1], (48, 32, 16))
    for first in range(0, out.shape[1], size):
        kept = dst[mv + slot + first : mv + slot + first + size, :]
        row = lax.broadcasted_iota(jnp.int32, kept.shape, 0) + first
        kept = jnp.where(row < end - start, kept, 0.0).astype(BF16)
        for i in range(out.shape[0]):
            out[i, first : first + size, :] = kept[:, i * block : (i + 1) * block]


def new_weights(tab, own, inner, outer, n, n_dp, rows, half):
    slot, width = own.shape
    mv = inner.shape[0]
    block = width // (2 * n_dp)

    def group(s, tab):
        return lax.rem(tab[3 * n + 2] + s, n_dp)

    return pl.pallas_call(
        functools.partial(weights_kernel, n),
        out_shape=jax.ShapeDtypeStruct((2, rows, width // 4), BF16),
        grid_spec=pltpu.PrefetchScalarGridSpec(
            num_scalar_prefetch=1,
            grid=(n_dp,),
            in_specs=[
                pl.BlockSpec((slot, block), lambda s, tab: (0, 2 * group(s, tab) + half)),
                pl.BlockSpec((mv, block), lambda s, tab: (0, group(s, tab))),
                pl.BlockSpec((mv, block), lambda s, tab: (0, group(s, tab))),
            ],
            out_specs=pl.BlockSpec((2, rows, block // 2), lambda s, tab: (0, 0, s)),
            scratch_shapes=[pltpu.VMEM((relayout_rows(slot, mv), block), F32)],
        ),
        compiler_params=params(),
        cost_estimate=cost(),
    )(tab, own, inner, outer)


def turned_kernel(piece, out):
    rows = piece.shape[1]
    for e in range(2):
        out[:, e * rows : (e + 1) * rows] = piece[e].astype(F32).T.astype(BF16)


def turned(piece):
    return pl.pallas_call(
        turned_kernel,
        out_shape=jax.ShapeDtypeStruct((piece.shape[2], 2 * piece.shape[1]), BF16),
        in_specs=[pl.BlockSpec(memory_space=pltpu.VMEM)],
        out_specs=pl.BlockSpec(memory_space=pltpu.VMEM),
        compiler_params=params(),
        cost_estimate=cost(),
    )(piece)


def forward_kernel(sent, tab, *refs):
    outs = refs[-4:-2] if sent else refs[-3:-2]
    pieces, (mine, other) = refs[: -4 - len(outs)], refs[-4 - len(outs) : -2 - len(outs)]
    hid, weights = refs[-2:]
    rows = mine.shape[1]
    tokens = pieces[0].shape[0]

    @pl.when(pl.program_id(0) == 0)
    def _():
        for i, piece in enumerate(pieces):
            hid[i * tokens : (i + 1) * tokens, :] = piece[...]

    weights[:rows, :] = mine[0]
    weights[rows:, :] = other[0]
    part = jnp.dot(hid[...], weights[...], preferred_element_type=F32).astype(BF16)
    for i in range(len(pieces)):
        block = part[i * tokens : (i + 1) * tokens, :]
        if not sent:
            outs[0][0, i] = block
        elif i < sent:
            outs[0][i, 0] = block
        else:
            outs[1][i - sent, 0] = block


def forward_chunk(tab, pieces, mine, other, sent, n_dp, at):
    tokens = pieces[0].shape[0]
    rows = mine.shape[1]
    block = mine.shape[2] // n_dp
    count = len(pieces)
    if sent:
        out_shape = [(sent, n_dp, tokens, block), (count - sent, n_dp, tokens, block)]
        out_specs = [pl.BlockSpec((shape[0], 1, tokens, block), lambda s: (0, s, 0, 0)) for shape in out_shape]
    else:
        out_shape = [(n_dp, count, tokens, block)]
        out_specs = [pl.BlockSpec((1, count, tokens, block), lambda s: (s, 0, 0, 0))]

    return pl.pallas_call(
        functools.partial(forward_kernel, sent),
        out_shape=[jax.ShapeDtypeStruct(shape, BF16) for shape in out_shape],
        grid=(n_dp,),
        in_specs=[SMEM]
        + [pl.BlockSpec(pieces[0].shape, lambda s: (0, 0))] * len(pieces)
        + [pl.BlockSpec((1, rows, block), lambda s: (at, 0, s))] * 2,
        out_specs=out_specs,
        scratch_shapes=[
            pltpu.VMEM((len(pieces) * tokens, 2 * rows), BF16),
            pltpu.VMEM((2 * rows, block), BF16),
        ],
        compiler_params=params(),
        cost_estimate=cost(),
    )(tab, *pieces, mine, other)


def fill_tokens(ht_refs, ht):
    tokens = ht_refs[0].shape[2]
    for i, ref in enumerate(ht_refs):
        ht[:, i * tokens : (i + 1) * tokens] = ref[0]


def fill_grads(parity, og_refs, places, og):
    refs = iter(og_refs)
    for at, flip, half, more, filled, rows in places:
        value = next(refs)[...] if filled else jnp.zeros((rows, og.shape[1]), og.dtype)
        if flip is None:
            og[at : at + rows, :] = value
        else:
            shift = (parity if flip == 0 else 1 - parity) * half + more
            og[pl.ds(pl.multiple_of(at + shift, rows), rows), :] = value


def partner_kernel(n, pieces, places, tab, *refs):
    ht_refs, og_refs, (out, ht, og) = refs[:pieces], refs[pieces:-3], refs[-3:]

    @pl.when(pl.program_id(0) == 0)
    def _():
        fill_tokens(ht_refs, ht)

    fill_grads(lax.rem(tab[3 * n + 2], 2), og_refs, places, og)
    out[...] = jnp.dot(ht[...], og[...], preferred_element_type=F32).astype(BF16)


def partner_grad(tab, pieces, grads, places, n):
    rows, tokens = pieces[0].shape[1:]
    width = grads[0].shape[1]
    block = min(width, 512)
    steps = width // block
    total = sum(place[5] for place in places)
    return pl.pallas_call(
        functools.partial(partner_kernel, n, len(pieces), places),
        out_shape=jax.ShapeDtypeStruct((rows, width), BF16),
        grid=(steps,),
        in_specs=[SMEM]
        + [pl.BlockSpec((1, rows, tokens), lambda i: (1, 0, 0))] * len(pieces)
        + [pl.BlockSpec((g.shape[0], block), lambda i: (0, i)) for g in grads],
        out_specs=pl.BlockSpec((rows, block), lambda i: (0, i)),
        scratch_shapes=[pltpu.VMEM((rows, total), BF16), pltpu.VMEM((total, block), BF16)],
        compiler_params=params(),
        cost_estimate=cost(),
    )(tab, *pieces, *grads)


def adam_kernel(n, pieces, grads, places, scale, aliased, relayed, tab, *refs):
    ht_refs, refs = refs[:pieces], refs[pieces:]
    og_refs, refs = refs[:grads], refs[grads:]
    rest, own, (inner0, inner1, outer0, outer1, inner_both, outer_both) = refs[0], refs[1:4], refs[4:10]
    refs = refs[10:]
    relay, refs = refs[:relayed], refs[relayed + aliased :]
    outs, ht, og, gradient, moved = refs[0:3], refs[3], refs[4], refs[5], refs[6:9]
    slot, mv = own[0].shape[0], inner0.shape[0]
    block = og.shape[1]
    even = lax.rem(pl.program_id(0) // 2, 2) == 0

    @pl.when(pl.program_id(0) == 0)
    def _():
        fill_tokens(ht_refs, ht)

    fill_grads(lax.rem(tab[3 * n + 2], 2), og_refs, places, og)
    odd = lax.rem(tab[3 * n + 1], 2) == 1
    middle = (tab[3 * n + 1] == n // 2 - 1) | (tab[3 * n + 1] == n // 2)
    inner = chosen(even, from_ref(inner0), from_ref(inner1))
    outer = chosen(even, from_ref(outer0), from_ref(outer1))
    relayout(tab, n, from_ref(own[0]), chosen(odd, inner, outer), chosen(odd, outer, inner), slot, mv, moved[0])
    for i in range(2):
        columns = slice(i * block, (i + 1) * block)
        inner, outer = from_ref(inner_both, columns), from_ref(outer_both, columns)
        if relay:
            outer = chosen(middle, from_ref(relay[0], columns), outer)
            inner = chosen(True, inner, inner)
        relayout(tab, n, from_ref(own[i + 1]), chosen(odd, inner, outer), chosen(odd, outer, inner), slot, mv, moved[i + 1])
    start, end = new_range(tab, n, tab[3 * n + 1])
    gradient[...] = jnp.dot(ht[...], og[...], preferred_element_type=F32)
    gradient[...] = (gradient[...] + rest[...].astype(F32)) * scale
    size = piece_rows(slot, (24, 16, 8))
    for first in range(0, slot, size):
        grad = gradient[first : first + size, :]
        at = mv + slot + first
        master, first_old, second_old = (ref[at : at + size, :] for ref in moved)
        first_next = 0.9 * first_old + 0.1 * grad
        second_next = 0.95 * second_old + 0.05 * grad * grad
        master_next = master - 0.001 * (first_next / (jnp.sqrt(second_next) + 1e-08) + 0.1 * master)
        live = lax.broadcasted_iota(jnp.int32, grad.shape, 0) + first < end - start
        for out, value in zip(outs, (master_next, first_next, second_next)):
            out[first : first + size, :] = jnp.where(live, value, 0.0)


def adam_part(tab, pieces, grads, places, rest, own, edge, both, outs, n, n_dp, scale, part, parts):
    rows, tokens = pieces[0].shape[1:]
    slot, width = own[0].shape
    mv = both[0].shape[0]
    block = width // (4 * n_dp)
    steps = width // parts // block
    total = sum(place[5] for place in places)
    inners, outers = edge

    def column(i):
        return 0, part * steps + i

    def first(i):
        return 0, (part * steps + i) // 4 * 2 + i % 2

    def inner_both(i):
        return 0, part * steps + i

    operands = [tab, *pieces, *grads, rest, *own, *inners, *outers, *both, *outs]
    return pl.pallas_call(
        functools.partial(adam_kernel, n, len(pieces), len(grads), places, scale, len(outs), len(both) - 2),
        out_shape=[jax.ShapeDtypeStruct((slot, width), F32)] * 3,
        grid=(steps,),
        in_specs=[SMEM]
        + [pl.BlockSpec((1, rows, tokens), lambda i: (0, 0, 0))] * len(pieces)
        + [pl.BlockSpec((g.shape[0], block), column) for g in grads]
        + [pl.BlockSpec((rows, block), column)]
        + [pl.BlockSpec((slot, block), column)] * 3
        + [pl.BlockSpec((mv, block), first)] * 4
        + [pl.BlockSpec((mv, 2 * block), inner_both)]
        + [pl.BlockSpec((mv, 2 * block), lambda i: (0, i))] * (len(both) - 1)
        + [pl.BlockSpec(memory_space=pl.ANY)] * len(outs),
        out_specs=[pl.BlockSpec((slot, block), column)] * 3,
        scratch_shapes=[
            pltpu.VMEM((rows, total), BF16),
            pltpu.VMEM((total, block), BF16),
            pltpu.VMEM((rows, block), F32),
        ]
        + [pltpu.VMEM((relayout_rows(slot, mv), block), F32)] * 3,
        input_output_aliases={len(operands) - 3 + i: i for i in range(3)} if outs else {},
        compiler_params=params(),
        cost_estimate=cost(),
    )(*operands)


def swap(value, mask):
    n = lax.axis_size("fsdp")
    return lax.ppermute(value, "fsdp", [(i, i ^ mask) for i in range(n)])


def swap_outer(value, middle=True):
    n = lax.axis_size("fsdp")
    pairs = [(i, i + 1 if i % 2 else i - 1) for i in range(1, n - 1)]
    return lax.ppermute(value, "fsdp", [(i, j) for i, j in pairs if middle or {i, j} != {3, 4}])


def relay_first(value):
    return lax.ppermute(value, "fsdp", [(3, 7), (4, 0)])


def relay_second(value):
    return lax.ppermute(value, "fsdp", [(7, 4), (0, 3)])


def turn(value, steps):
    n = lax.axis_size("dp")
    return lax.ppermute(value, "dp", [(i, (i + steps) % n) for i in range(n)])


def stage(*values):
    return lax.optimization_barrier(values)


def add(a, b):
    return (a.astype(F32) + b.astype(F32)).astype(BF16)


def local(gate, up, out_grad, master_old, moment1_old, moment2_old, old_bounds, new_bounds, rank_map):
    n, n_dp = lax.axis_size("fsdp"), lax.axis_size("dp")
    groups = n // 2
    square = groups == 4
    chunks, parts = 4, 4
    tokens, block_rows = gate.shape
    slot, width = master_old.shape[1:]
    rows = round_up(slot, 16)
    mv = round_up((block_rows // n + 1) // 2, 16)
    scale = 1.0 / math.sqrt(tokens * n)
    index = jnp.stack([lax.axis_index("fsdp"), lax.axis_index("dp")]).astype(jnp.int32)
    tab = jnp.concatenate([old_bounds[0], new_bounds[0], rank_map[0], index])
    own = [master_old[0], moment1_old[0], moment2_old[0]]
    half = tokens // 2
    parity = lax.rem(lax.axis_index("dp"), 2)

    block = width // (2 * n_dp)
    small = block // 2
    steps = width // parts // small
    order = [2, 3, 0, 1] if square else list(range(1, groups)) + [0]
    sent = 2 if square else groups - 1

    def flip(value):
        return lax.ppermute(value, "dp", [(i, i ^ 1) for i in range(n_dp)])

    def forward(chunk):
        mine, other = weights[chunk // 2]
        by_dp = square and chunk == 1
        return forward_chunk(tab, [tokens_first[i] for i in order], mine, other, 0 if by_dp else sent, n_dp, chunk % 2)

    def first_sum(chunk):
        send = sends[chunk]
        if square:
            return [swap(send, 4)]
        return [swap(send[rel - 1], 2 * rel) for rel in range(1, groups)]

    def second_sum(chunk):
        return swap(add(keeps[chunk][1], came[chunk][0][1]), 2) if square else tab

    def summed(chunk, passed):
        total = keeps[chunk][0].astype(F32)
        if square:
            return total + came[chunk][0][0].astype(F32) + passed.astype(F32)
        for value in came[chunk]:
            total = total + value.astype(F32)
        return total

    def over_dp(total):
        low = total.astype(BF16)
        out = total[0]
        for turned_by in range(1, n_dp):
            out = out + turn(low[turned_by], turned_by).astype(F32)
        return out

    def step(part, outs):
        moved = (moving_inner, *moved_outer[part])
        return list(
            adam_part(tab, tokens_of, grads, places, partner, own, (inners, outers), moved, outs, n, n_dp, scale, part, parts)
        )

    def master_edges(tab, h):
        inner, outer = edges(tab, own[:1], n, mv, block, [[(2 * j + h) * block for j in range(n_dp)]])
        return inner, outer

    quarter = half // 2
    inner, outer = master_edges(tab, 0)
    tab, inner, outer, out_grad = stage(tab, inner, outer, out_grad)
    mine_grad = lax.dynamic_slice_in_dim(out_grad, parity * half, half, 0)
    quarters = [lax.dynamic_slice_in_dim(out_grad, parity * half + at, quarter, 0) for at in (0, quarter)]
    inners, outers = [swap(inner, 1)], [swap_outer(outer)]
    inner, outer = master_edges(tab, 1)
    inners.append(inner)
    outers.append(outer)
    windows = list(hidden_windows(tab, gate, up, n, rows))
    moving = list(
        edges(
            tab,
            own[1:],
            n,
            mv,
            small,
            [[(part * steps + i) * small for i in range(steps)] for part in range(parts)],
        )
    )
    grad_y = [swap(quarters[0], 4)] if square else []
    tab, inners, outers, mine_grad, quarters, grad_y, windows, moving = stage(
        tab, inners, outers, mine_grad, quarters, grad_y, windows, moving
    )

    inners, outers, moving, grad_y = list(inners), list(outers), list(moving), list(grad_y)
    outers[1] = swap_outer(outers[1])
    inners[1] = swap(inners[1], 1)
    flips_y = []
    if square:
        grad_y.append(swap(quarters[1], 4))
        flips_y.append(flip(grad_y[0]))
    moving_inner = swap(moving[0], 1)
    mine = new_weights(tab, own[0], inners[0], outers[0], n, n_dp, rows, 0)
    tab, inners, outers, mine_grad, grad_y, flips_y, windows, moving, moving_inner, mine = stage(
        tab, inners, outers, mine_grad, grad_y, flips_y, windows, moving, moving_inner, mine
    )

    pieces, flips_y = list(windows), list(flips_y)
    for rel in range(1, groups):
        pieces[rel] = swap(pieces[rel], 2 * rel)
    weights = [(mine, swap(mine, 1))]
    if square:
        flips_y.append(flip(grad_y[1]))
    mine = new_weights(tab, own[0], inners[1], outers[1], n, n_dp, rows, 1)
    tokens_first = [turned(pieces[0])]
    tab, mine_grad, flips_y, moving, pieces, weights, mine, tokens_first = stage(
        tab, mine_grad, flips_y, moving, pieces, weights, mine, tokens_first
    )

    weights = list(weights) + [(mine, swap(mine, 1))]
    tokens_first = list(tokens_first) + [turned(piece) for piece in pieces[1:]]
    sends, keeps, came, totals = [None] * chunks, [None] * chunks, [None] * chunks, [None] * chunks
    sends[0], keeps[0] = forward(0)
    if square:
        (last,) = forward(1)
    else:
        sends[1], keeps[1] = forward(1)
        last = tab
    grad_x = swap(mine_grad, 2) if square else mine_grad
    relays = [relay_first(moving[2]), relay_first(moving[4])] if square else []
    tab, grad_x, moving, weights, sends, keeps, tokens_first, relays, last = stage(
        tab, grad_x, moving, weights, sends, keeps, tokens_first, relays, last
    )

    sends, keeps, relays = list(sends), list(keeps), list(relays)
    moved_outer = [(swap_outer(moving[1]),)]
    if square:
        relays[0] = relay_second(relays[0])
        grad_g, flip_x = swap(grad_x, 4), flip(grad_x)
    else:
        grad_g, flip_x = grad_x, grad_x
    turns = [turn(last[i], i) for i in range(2, n_dp, 2)] if square else []
    sends[2], keeps[2] = forward(2)
    sends[3], keeps[3] = forward(3)
    tab, grad_x, grad_g, flip_x, moving, moved_outer, sends, keeps, relays, turns, last = stage(
        tab, grad_x, grad_g, flip_x, moving, moved_outer, sends, keeps, relays, turns, last
    )

    sends, keeps, moved_outer, relays = list(sends), list(keeps), list(moved_outer), list(relays)
    moved_outer.append((swap_outer(moving[2], not square), *relays[:1]))
    came[0] = first_sum(0)
    if square:
        relays[1] = relay_second(relays[1])
    flip_g = flip(grad_g) if square else grad_g
    tokens_of = pieces
    if square:
        grads = [out_grad, grad_x, *grad_y, grad_g, flip_x, *flips_y]
        places = [(0, None, tokens, 0, True, tokens)]
        for which in range(2):
            places += [(tokens, which, half, 0, True, half)]
            places += [(2 * tokens, which, half, more, True, quarter) for more in (0, quarter)]
            places += [(3 * tokens, which, half, 0, which == 0, half)]
        tokens_of = pieces + [swap(pieces[3][1], 1)[None]]
    else:
        grads = [out_grad] + [swap(out_grad, 2 * rel) for rel in range(1, groups)]
        places = [(i * tokens, None, tokens, 0, True, tokens) for i in range(groups)]
    partner = partner_grad(tab, pieces, grads, places, n)
    odd_turns = [last[i] for i in range(1, n_dp, 2)] if square else []
    tab, flip_g, moving, moved_outer, sends, keeps, came, relays, tokens_of, partner, odd_turns = stage(
        tab, flip_g, moving, moved_outer, sends, keeps, came, relays, tokens_of, partner, odd_turns
    )

    keeps, came, moved_outer = list(keeps), list(came), list(moved_outer)
    moved_outer.append((swap_outer(moving[3]),))
    came[2] = first_sum(2)
    totals[0] = second_sum(0)
    partner = swap(partner, 1)
    if square:
        partner, flip_core, tab = stage(partner, swap(flip_g, 1), tab)
        grads = grads + [flip_g, flip_core]
        places = places[:-1] + [(3 * tokens, 1, half, 0, True, half)]
        places += [(4 * tokens, 0, half, 0, False, half), (4 * tokens, 1, half, 0, True, half)]
    else:
        partner, tab = stage(partner, tab)
    outs = step(1, step(0, []))
    tab, moving, moved_outer, sends, came, totals, outs, last = stage(
        tab, moving, moved_outer, sends, came, totals, outs, last
    )

    came, totals, moved_outer = list(came), list(totals), list(moved_outer)
    moved_outer.append((swap_outer(moving[4], not square), *relays[1:]))
    came[3] = first_sum(3)
    totals[2] = second_sum(2)
    turns = list(turns)
    if square:
        turns += [turn(value, 2 * i + 1) for i, value in enumerate(odd_turns)]
    outs = step(2, list(outs))
    tab, moved_outer, sends, came, totals, outs, turns = stage(
        tab, moved_outer, sends, came, totals, outs, turns
    )

    came, totals = list(came), list(totals)
    totals[3] = second_sum(3)
    if square:
        total = last[0].astype(F32)
        for value in turns:
            total = total + value.astype(F32)
        came[1] = [swap(total[:2].astype(BF16), 4)]
        keeps[1] = total[2:]
    else:
        came[1] = first_sum(1)
    both = over_dp(jnp.stack([summed(i, totals[i]) for i in (0, 2)], axis=1))
    outs = step(3, list(outs))
    tab, came, totals, outs = stage(tab, came, totals, list(outs))

    totals = list(totals)
    total = summed(1, second_sum(1))
    results = [both[0], total if square else over_dp(total), both[1], over_dp(summed(3, totals[3]))]
    mlp_out = jnp.concatenate(results, axis=1)
    return mlp_out, outs[0][None], outs[1][None], outs[2][None]


def solution(mesh):
    placed = (
        P("fsdp", "dp"),
        P("fsdp", "dp"),
        P("fsdp", None),
        P("dp", "fsdp", None),
        P("dp", "fsdp", None),
        P("dp", "fsdp", None),
        P("dp", None),
        P("dp", None),
        P("dp", None),
    )
    return jax.shard_map(
        local,
        mesh=mesh,
        in_specs=placed,
        out_specs=(
            P("fsdp", "dp"),
            P("dp", "fsdp", None),
            P("dp", "fsdp", None),
            P("dp", "fsdp", None),
        ),
        check_vma=False,
    )
```
